512 devices in a mesh: dp: 128 (over z, y, core), proto: 4 (over x).
Axes of the slice: x: 4, y: 8, z: 8, core: 2. Of those that a mesh axis runs over, the one named last changes fastest.
Arguments:
- view_embed: bfloat16 [32768, 128], P('dp'), may hold values from -60 to 60
- pair_slot: int32 [16384, 2], P('dp'), may hold values from 0 to 255, as said below
- prototypes: bfloat16 [32768, 128], P('proto'), may hold values from -40 to 40
Outputs:
- possession_loss: float32 [16384], P('dp')
- proto_grad: bfloat16 [32768, 128], P('proto')
The draws below stay inside these ranges and needn't reach their ends.
Inputs may be any that keep to these rules, and one draw needn't show every extreme that they name: `pair_slot`: within each aligned block of 128 possessions, the 256 entries name each of that block's view slots once.
All inputs are finite; a program needn't handle non-finite values.
Results may differ from the reference program's by a relative error of at most 0.0063.
Values may be sent and summed in bfloat16 or wider, within the bound.
A program may use at most 64 MiB of HBM per device.

```python
import math
import jax
import jax.numpy as jnp
from jax import lax

D = 128
ROWS_DEV = 128
SINK_ITERS = 3
POSS = 16384
PROTOS = 32768


def proto_base(key):
    gauss_rows = jax.random.normal(jax.random.fold_in(key, 101), (PROTOS, D), jnp.float32)
    return jnp.clip(gauss_rows, -4.0, 4.0)


def draw_prototypes(key, part):
    gauss_rows = proto_base(key)
    key = jax.random.fold_in(key, 1)
    row_gain = jnp.exp(jax.random.uniform(jax.random.fold_in(key, 2), (PROTOS, 1), jnp.float32, 0.0, math.log(10.0)))
    scaled = gauss_rows * row_gain
    return jnp.clip(scaled, -40.0, 40.0).astype(jnp.bfloat16)


def draw_view_embed(key, part):
    gauss_rows = proto_base(key)
    key = jax.random.fold_in(key, 7)
    chosen_rows = jax.random.randint(jax.random.fold_in(key, 1), (2 * POSS, 2), 0, PROTOS)
    weights = jax.random.uniform(jax.random.fold_in(key, 2), (2 * POSS, 2), jnp.float32, 0.3, 1.0)
    mixed = gauss_rows[chosen_rows[:, 0]] * weights[:, :1] + 0.5 * gauss_rows[chosen_rows[:, 1]] * weights[:, 1:]
    jitter = jax.random.normal(jax.random.fold_in(key, 3), (2 * POSS, D), jnp.float32) * 0.6
    row_gain = jnp.exp(jax.random.uniform(jax.random.fold_in(key, 4), (2 * POSS, 1), jnp.float32, 0.0, math.log(10.0)))
    return jnp.clip((mixed + jitter) * row_gain, -60.0, 60.0).astype(jnp.bfloat16)


def draw_pair_slot(key, part):
    key = jax.random.fold_in(key, 5)
    subkeys = jax.random.split(key, POSS // ROWS_DEV)

    def shuffle(subkey):
        return jax.random.permutation(subkey, 2 * ROWS_DEV)
    orders = jax.vmap(shuffle)(subkeys)
    return orders.reshape(POSS, 2).astype(jnp.int32)


def setup_inputs(seed: int = 0) -> dict:
    keys = jax.random.split(jax.random.key(seed), 4)
    return {
        "view_embed": draw_view_embed(jax.random.fold_in(keys[3], 71), 0),
        "pair_slot": draw_pair_slot(jax.random.fold_in(keys[3], 71), 0),
        "prototypes": draw_prototypes(jax.random.fold_in(keys[3], 71), 0),
    }


sink_eps = 0.05
temper = 0.1
norm_eps = 1e-06

def unit_rows(matrix):
    widened = matrix.astype(jnp.float32)
    factor = lax.rsqrt(lax.optimization_barrier(jnp.sum(widened * widened, axis=-1, keepdims=True)) + norm_eps)
    return (widened * factor).astype(jnp.bfloat16)

def reference(view_embed, pair_slot, prototypes):
    offsets = jnp.arange(POSS, dtype=jnp.int32) // ROWS_DEV * (2 * ROWS_DEV)
    chosen = view_embed[(pair_slot + offsets[:, None]).astype(jnp.int32)]
    unit_z = unit_rows(jnp.transpose(chosen, (1, 0, 2)).reshape(2 * POSS, D))
    wide_z = unit_z.astype(jnp.float32)
    block_k = math.gcd(PROTOS, 1024)
    blocks = PROTOS // block_k
    proto_tiles = unit_rows(prototypes).reshape(blocks, block_k, D)

    def scores_of(proto_tile):
        return jnp.dot(wide_z, proto_tile.astype(jnp.float32).T, preferred_element_type=jnp.float32)

    def column_terms(row_scale):

        def column_block(proto_tile):
            weighted = row_scale[:, None] * jnp.exp(scores_of(proto_tile) / sink_eps)
            return lax.optimization_barrier(jnp.sum(weighted.reshape(2, POSS, block_k), axis=1))
        parts = lax.map(column_block, proto_tiles)
        return jnp.transpose(parts, (1, 0, 2)).reshape(2, PROTOS)

    def column_layout(col_scale):
        return jnp.transpose(col_scale.reshape(2, blocks, block_k), (1, 0, 2))

    def row_terms(col_scale, is_last):

        def advance(running, element):
            proto_tile, scale_tile = element
            scores = scores_of(proto_tile)
            exponent = jnp.exp(scores / sink_eps).reshape(2, POSS, block_k)
            row_part = running[0] + lax.optimization_barrier(jnp.sum(exponent * scale_tile[:, None, :], axis=2)).reshape(2 * POSS)
            if is_last:
                spread = running[1] + lax.optimization_barrier(jnp.sum(jnp.exp(scores / temper), axis=1))
            else:
                spread = running[1]
            return ((row_part, spread), None)
        initial = (jnp.zeros((2 * POSS,), jnp.float32), jnp.zeros((2 * POSS,), jnp.float32))
        totals, unused = lax.scan(advance, initial, (proto_tiles, column_layout(col_scale)))
        return totals
    row_scale = jnp.ones((2 * POSS,), jnp.float32)
    col_scale = row_scale
    spread_total = row_scale
    for iteration in range(SINK_ITERS):
        is_last = iteration == SINK_ITERS - 1
        col_scale = 1.0 / column_terms(row_scale)
        row_total, spread_total = row_terms(col_scale, is_last)
        row_scale = 1.0 / row_total
    log_total = jnp.log(spread_total).reshape(2, POSS)

    def final_step(running, element):
        proto_tile, scale_tile = element
        scores = scores_of(proto_tile).reshape(2, POSS, block_k)
        exponent = jnp.exp(scores / sink_eps)
        assign = row_scale.reshape(2, POSS)[:, :, None] * exponent * scale_tile[:, None, :]
        predict = jnp.exp(scores / temper - log_total[:, :, None])
        swapped = assign[::-1]
        coefficient = ((predict - swapped) / temper).astype(jnp.bfloat16).reshape(2 * POSS, block_k)
        grad_tile = jnp.dot(coefficient.astype(jnp.float32).T, wide_z, preferred_element_type=jnp.float32)
        cross_part = running[0] + lax.optimization_barrier(jnp.sum(swapped * scores, axis=2))
        mass_part = running[1] + lax.optimization_barrier(jnp.sum(swapped, axis=2))
        return ((cross_part, mass_part), grad_tile)
    initial = (jnp.zeros((2, POSS), jnp.float32), jnp.zeros((2, POSS), jnp.float32))
    (cross_total, mass_total), pieces = lax.scan(final_step, initial, (proto_tiles, column_layout(col_scale)))
    proto_grad = pieces.reshape(PROTOS, D).astype(jnp.bfloat16)
    possession_loss = -0.5 * lax.optimization_barrier(jnp.sum(cross_total / temper - log_total * mass_total, axis=0))
    return (possession_loss, proto_grad)
```

```python
import jax
import jax.numpy as jnp
from jax import lax
from jax.experimental import pallas as pl
from jax.experimental.pallas import tpu as pltpu
from jax.sharding import PartitionSpec as P

MESH = pl.DeviceIdType.MESH
F32 = jnp.float32
BF16 = jnp.bfloat16
X, Y, Z = 4, 8, 8
L = 128
ITERS = 3
EPS = 1e-6


def coords():
    dp = lax.axis_index("dp")
    return lax.axis_index("proto"), (dp // 2) % Y, dp // (2 * Y), dp % 2


def device(x, y, z, c):
    return ((z * Y + y) * 2 + c, x)


def across(row):
    return jnp.transpose(jnp.broadcast_to(row, (L, L)))


def unit(wide):
    return (wide * lax.rsqrt(jnp.sum(wide * wide, axis=-1, keepdims=True) + EPS)).astype(BF16)


def kernel(
    view_ref, slot_ref, proto_ref, loss_ref, grad_ref,
    raw, unit_c, z_own, z_mine, z_other, expo, soft, weighted, z_scaled, grad_soft,
    col_part, col_send, col_got, col_scale, row_got, row_part, row_scale,
    half_send, half_got, half_own, half_out, piece_got, shard, whole, loss_rows, loss_send, loss_got,
    raw_sem, z_send, z_recv, o_send, o_recv, col_ssem, col_rsem, row_ssem, row_rsem,
    half_ssem, half_rsem, piece_ssem, piece_rsem, all_ssem, all_rsem, near_ssem, near_rsem,
    pass_ssem, pass_rsem, loss_ssem, loss_rsem, out_sem,
):
    x, y, z, c = coords()
    yb, zb, yh, zh = y % 2, z % 2, y // 2, z // 2
    quad = zb * 2 + yb
    row_me = (x * 2 + yb) * 2 + zb
    col_me = zh * (Y // 2) + yh
    n_row, n_col = X * 4, (Y // 2) * (Z // 2)
    sibling = device(x, y, z, 1 - c)

    def row_peer(step):
        t = (row_me + step) % n_row
        return device(t // 4, yh * 2 + (t // 2) % 2, zh * 2 + t % 2, c)

    def col_peer(step):
        t = (col_me + step) % n_col
        return t, device(x, (t % (Y // 2)) * 2 + yb, (t // (Y // 2)) * 2 + zb, c)

    def quad_peer(step, core):
        t = (quad + step) % 4
        return device(x, yh * 2 + t % 2, zh * 2 + t // 2, core)

    def near(dy, dz):
        return device(x, (y + dy) % Y, (z + dz) % Z, c)

    near_steps = [(1, 0), (-1, 0), (0, 1), (0, -1), (1, 1), (1, -1), (-1, 1), (-1, -1)]

    barrier = pltpu.get_barrier_semaphore()

    def hail(target):
        pl.semaphore_signal(barrier, inc=1, device_id=target, device_id_type=MESH)

    hail(sibling)
    for step in range(1, 4):
        hail(quad_peer(step, 0))
        hail(quad_peer(step, 1))
    for dy, dz in near_steps:
        hail(near(dy, dz))

    def hail_groups(step, unused):
        hail(row_peer(step))
        hail(col_peer(step)[1])
        return unused

    lax.fori_loop(1, 16, hail_groups, 0)

    fetch = pltpu.make_async_copy(proto_ref.at[pl.ds(quad * 2048, 2048)], raw, raw_sem)
    fetch.start()

    lanes = lax.broadcasted_iota(jnp.int32, (L, 2 * L), 1)
    for v in range(2):
        pick = (slot_ref[:, v : v + 1] == lanes).astype(F32).astype(BF16)
        z_own[v] = unit(jnp.dot(pick, view_ref[...], preferred_element_type=F32))
    pl.semaphore_wait(barrier, 45)

    place = quad * 2 + c
    z_mine[place] = z_own[c]
    pltpu.make_async_remote_copy(
        z_own.at[1 - c], z_mine.at[place], z_send, z_recv, device_id=sibling, device_id_type=MESH
    ).start()
    for step in range(1, 4):
        for core in range(2):
            pltpu.make_async_remote_copy(
                z_own.at[core], z_mine.at[place], z_send, z_recv,
                device_id=quad_peer(step, core), device_id_type=MESH,
            ).start()

    fetch.wait()

    def normalise(b, unused):
        unit_c[b] = unit(raw[pl.ds(b * L, L)].astype(F32))
        return unused

    lax.fori_loop(0, 16, normalise, 0)

    seven = z_mine.at[pl.ds(0, 7)]
    pltpu.make_async_copy(seven, seven, z_recv).wait()
    pltpu.make_async_copy(seven, seven, z_send).wait()
    to_other = pltpu.make_async_remote_copy(
        z_mine, z_other, o_send, o_recv, device_id=sibling, device_id_type=MESH
    )
    to_other.start()

    def dot_t(a, b):
        return lax.dot_general(a, b, (((1,), (1,)), ((), ())), preferred_element_type=F32)

    def fold(block):
        return jnp.sum(block.reshape(16, 8, block.shape[-1]), axis=0)

    def lay(part):
        row = jnp.sum(part, axis=0, keepdims=True)
        return jnp.concatenate([row[:, t * L : (t + 1) * L] for t in range(8)], axis=0)

    rows_z = z_mine[...].reshape(1024, L)

    def first(b, total):
        scores = dot_t(unit_c[b], rows_z)
        power = jnp.exp(scores * 10.0)
        soft[b] = power.astype(BF16)
        square = power * power
        expo[b] = square
        wide = square[:, 0:L]
        for t in range(1, 8):
            wide = wide + square[:, t * L : (t + 1) * L]
        col_part[pl.ds(b, 1)] = jnp.sum(jnp.transpose(wide), axis=0, keepdims=True)
        return total + fold(power)

    total_part = lax.fori_loop(0, 16, first, jnp.zeros((8, 1024), F32))

    def exchange_columns(it):
        col_send[it] = col_part[...].astype(BF16)
        got = col_got.at[it]
        got[col_me] = col_send[it]

        def send(step, unused):
            pltpu.make_async_remote_copy(
                col_send.at[it], got.at[col_me], col_ssem.at[it], col_rsem.at[it],
                device_id=col_peer(step)[1], device_id_type=MESH,
            ).start()
            return unused

        lax.fori_loop(1, n_col, send, 0)
        most = got.at[pl.ds(0, n_col - 1)]
        pltpu.make_async_copy(most, most, col_rsem.at[it]).wait()
        total = got[0].astype(F32)
        for m in range(1, n_col):
            total = total + got[m].astype(F32)
        col_scale[...] = 1.0 / total

    def exchange_rows(it, parts):
        row_part[it, 0:8] = parts[0]
        row_part[it, 8:16] = parts[1]
        got = row_got.at[it]
        got[row_me] = row_part[it]

        def send(step, unused):
            pltpu.make_async_remote_copy(
                row_part.at[it], got.at[row_me], row_ssem.at[it], row_rsem.at[it],
                device_id=row_peer(step), device_id_type=MESH,
            ).start()
            return unused

        lax.fori_loop(1, n_row, send, 0)
        most = got.at[pl.ds(0, n_row - 1)]
        pltpu.make_async_copy(most, most, row_rsem.at[it]).wait()
        total = got[0]
        for m in range(1, n_row):
            total = total + got[m]
        row_scale[...] = 1.0 / total[0:8]
        return total[0:8], total[8:16]

    def row_pass(b, acc):
        scale = across(col_scale[pl.ds(b, 1)])
        parts = [fold(expo[b, :, t * L : (t + 1) * L] * scale) for t in range(8)]
        return acc + jnp.concatenate(parts, axis=1)

    def col_pass(b, unused):
        wide = expo[b, :, 0:L] * row_scale[0:1]
        for t in range(1, 8):
            wide = wide + expo[b, :, t * L : (t + 1) * L] * row_scale[t : t + 1]
        col_part[pl.ds(b, 1)] = jnp.sum(jnp.transpose(wide), axis=0, keepdims=True)
        return unused

    zero = jnp.zeros((8, 1024), F32)

    exchange_columns(0)
    acc = lax.fori_loop(0, 16, row_pass, zero)
    total = exchange_rows(0, (lay(acc), lay(total_part)))[1]
    log_total = jnp.log(total)
    gain = 10.0 / total
    lax.fori_loop(0, 16, col_pass, 0)
    exchange_columns(1)
    acc = lax.fori_loop(0, 16, row_pass, zero)
    exchange_rows(1, (lay(acc), jnp.zeros((8, L), F32)))
    lax.fori_loop(0, 16, col_pass, 0)
    exchange_columns(2)

    for t in range(8):
        z_scaled[t] = (z_mine[t].astype(F32) * across(gain[t : t + 1])).astype(BF16)
    scaled = z_scaled[...].reshape(1024, L)

    def soft_grad(b, unused):
        grad_soft[b] = jnp.dot(soft[b], scaled, preferred_element_type=F32)
        return unused

    lax.fori_loop(0, 16, soft_grad, 0)
    to_other.wait()
    rows_o = z_other[...].reshape(1024, L)

    def last_pass(b, carry):
        acc, cross = carry
        scale = across(col_scale[pl.ds(b, 1)])
        other = dot_t(unit_c[b], rows_o)
        parts, crossed = [], []
        for t in range(8):
            here = expo[b, :, t * L : (t + 1) * L] * scale
            weighted[b, :, t * L : (t + 1) * L] = here.astype(BF16)
            parts.append(fold(here))
            crossed.append(fold(here * other[:, t * L : (t + 1) * L]))
        return acc + jnp.concatenate(parts, axis=1), cross + jnp.concatenate(crossed, axis=1)

    acc, cross = lax.fori_loop(0, 16, last_pass, (zero, zero))
    row_total, cross = exchange_rows(2, (lay(acc), lay(cross)))

    for t in range(8):
        z_scaled[t] = (z_other[t].astype(F32) * across(row_scale[t : t + 1] * 10.0)).astype(BF16)
    scaled = z_scaled[...].reshape(1024, L)

    def grad_block(b):
        return grad_soft[b] - jnp.dot(weighted[b], scaled, preferred_element_type=F32)

    def away(b, unused):
        half_send[b] = grad_block((1 - c) * 8 + b).astype(BF16)
        return unused

    lax.fori_loop(0, 8, away, 0)
    half = pltpu.make_async_remote_copy(
        half_send, half_got, half_ssem, half_rsem, device_id=sibling, device_id_type=MESH
    )
    half.start()

    def stay(b, unused):
        half_own[b] = grad_block(c * 8 + b)
        return unused

    lax.fori_loop(0, 8, stay, 0)

    scale = row_scale[...]
    loss_rows[0] = log_total
    loss_rows[1] = scale * cross
    loss_rows[2] = scale * row_total
    theirs = pl.ds(quad * 2 + (1 - c), 1)
    loss_send[...] = jnp.zeros((8, L), F32)
    for n in range(3):
        loss_send[n : n + 1] = loss_rows[n, theirs]
    loss_copy = pltpu.make_async_remote_copy(
        loss_send, loss_got, loss_ssem, loss_rsem, device_id=sibling, device_id_type=MESH
    )
    loss_copy.start()

    half.wait()
    half_out[...] = (half_own[...] + half_got[...].astype(F32)).astype(BF16).reshape(16, 64, L)

    def send_piece(step, unused):
        t, target = col_peer(step)
        pltpu.make_async_remote_copy(
            half_out.at[t], piece_got.at[col_me], piece_ssem, piece_rsem,
            device_id=target, device_id_type=MESH,
        ).start()
        return unused

    lax.fori_loop(1, n_col, send_piece, 0)
    piece_got[col_me] = half_out[col_me]

    loss_copy.wait()
    mine = pl.ds(place, 1)
    own_log, own_cross, own_mass = [loss_rows[n, mine] for n in range(3)]
    sib_log, sib_cross, sib_mass = [loss_got[n : n + 1] for n in range(3)]
    loss_ref[...] = -0.5 * (
        (own_cross + sib_cross) * 10.0 - own_log * sib_mass - sib_log * own_mass
    )

    most = piece_got.at[pl.ds(0, n_col - 1)]
    pltpu.make_async_copy(most, most, piece_rsem).wait()
    summed = piece_got[0].astype(F32)
    for m in range(1, n_col):
        summed = summed + piece_got[m].astype(F32)
    shard[...] = summed.astype(BF16)

    spot = whole.at[place]
    spot[pl.ds(col_me * 64, 64)] = shard[...]

    def send_shard(step, unused):
        pltpu.make_async_remote_copy(
            shard, spot.at[pl.ds(col_me * 64, 64)], all_ssem, all_rsem,
            device_id=col_peer(step)[1], device_id_type=MESH,
        ).start()
        return unused

    lax.fori_loop(1, n_col, send_shard, 0)
    bulk = spot.at[pl.ds(0, 960)]
    pltpu.make_async_copy(bulk, bulk, all_rsem).wait()

    kinds = [0, 0, 1, 1, 2, 2, 2, 2]
    starts = [0, 512, 0, 512, 0, 256, 512, 768]
    for (dy, dz), kind, start in zip(near_steps, kinds, starts):
        part = spot.at[pl.ds(start, 256 if kind == 2 else 512)]
        pltpu.make_async_remote_copy(
            part, part, near_ssem.at[kind], near_rsem.at[kind],
            device_id=near(dy, dz), device_id_type=MESH,
        ).start()

    def hand_over(which, sem):
        part = whole.at[which]
        pltpu.make_async_remote_copy(
            part, part, pass_ssem.at[sem], pass_rsem.at[sem], device_id=sibling, device_id_type=MESH
        ).start()

    def write_out(which, sem):
        pltpu.make_async_copy(
            whole.at[which], grad_ref.at[pl.ds(which * 1024, 1024)], out_sem.at[sem]
        ).start()

    hand_over(place, 0)
    write_out(place, 0)
    others = [zb * 2 + (1 - yb), (1 - zb) * 2 + yb, (1 - zb) * 2 + (1 - yb)]
    for kind, q in enumerate(others):
        got = whole.at[q * 2 + c]
        pltpu.make_async_copy(got, got, near_rsem.at[kind]).wait()
        hand_over(q * 2 + c, kind + 1)
        write_out(q * 2 + c, kind + 1)
    for n, q in enumerate([quad] + others):
        got = whole.at[q * 2 + (1 - c)]
        pltpu.make_async_copy(got, got, pass_rsem.at[n]).wait()
        write_out(q * 2 + (1 - c), n + 4)

    one = whole.at[0]
    for n in range(8):
        pltpu.make_async_copy(one, one, out_sem.at[n]).wait()
    for n in range(4):
        pltpu.make_async_copy(one, one, pass_ssem.at[n]).wait()
    for n in range(3):
        pltpu.make_async_copy(one, one, near_ssem.at[n]).wait()
    pltpu.make_async_copy(bulk, bulk, all_ssem).wait()
    pltpu.make_async_copy(most, most, piece_ssem).wait()
    for it in range(ITERS):
        part = col_got.at[it, pl.ds(0, n_col - 1)]
        pltpu.make_async_copy(part, part, col_ssem.at[it]).wait()
        part = row_got.at[it, pl.ds(0, n_row - 1)]
        pltpu.make_async_copy(part, part, row_ssem.at[it]).wait()


def local(view_embed, pair_slot, prototypes):
    vmem, dma = pltpu.VMEM, pltpu.SemaphoreType.DMA
    scratch = [
        vmem((2048, L), BF16),
        vmem((16, L, L), BF16),
        vmem((2, L, L), BF16),
        vmem((8, L, L), BF16),
        vmem((8, L, L), BF16),
        vmem((16, L, 1024), F32),
        vmem((16, L, 1024), BF16),
        vmem((16, L, 1024), BF16),
        vmem((8, L, L), BF16),
        vmem((16, L, L), F32),
        vmem((16, L), F32),
        vmem((ITERS, 16, L), BF16),
        vmem((ITERS, 16, 16, L), BF16),
        vmem((16, L), F32),
        vmem((ITERS, 16, 16, L), F32),
        vmem((ITERS, 16, L), F32),
        vmem((8, L), F32),
        vmem((8, L, L), BF16),
        vmem((8, L, L), BF16),
        vmem((8, L, L), F32),
        vmem((16, 64, L), BF16),
        vmem((16, 64, L), BF16),
        vmem((64, L), BF16),
        vmem((8, 1024, L), BF16),
        vmem((3, 8, L), F32),
        vmem((8, L), F32),
        vmem((8, L), F32),
        dma, dma, dma, dma, dma,
        dma((ITERS,)), dma((ITERS,)), dma((ITERS,)), dma((ITERS,)),
        dma, dma, dma, dma, dma, dma,
        dma((3,)), dma((3,)), dma((4,)), dma((4,)),
        dma, dma, dma((8,)),
    ]
    loss, grad = pl.pallas_call(
        kernel,
        out_shape=[
            jax.ShapeDtypeStruct((1, L), F32),
            jax.ShapeDtypeStruct((8192, L), BF16),
        ],
        in_specs=[
            pl.BlockSpec(memory_space=pltpu.VMEM),
            pl.BlockSpec(memory_space=pltpu.VMEM),
            pl.BlockSpec(memory_space=pl.ANY),
        ],
        out_specs=[
            pl.BlockSpec(memory_space=pltpu.VMEM),
            pl.BlockSpec(memory_space=pl.ANY),
        ],
        scratch_shapes=scratch,
        compiler_params=pltpu.CompilerParams(
            collective_id=0, has_side_effects=True, vmem_limit_bytes=48 << 20
        ),
        name="swav_step",
    )(view_embed, pair_slot, prototypes)
    return loss.reshape(L), grad


def solution(mesh):
    placed = (P("dp", None), P("dp", None), P("proto", None))
    return jax.shard_map(
        local, mesh=mesh, in_specs=placed, out_specs=(P("dp"), P("proto", None)), check_vma=False
    )
```

```python
import math

import jax
import jax.numpy as jnp
from jax import lax
from jax.experimental import pallas as pl
from jax.experimental.pallas import tpu as pltpu
from jax.sharding import PartitionSpec as P

MESH = pl.DeviceIdType.MESH
F32 = jnp.float32
BF16 = jnp.bfloat16
X, Y, Z = 4, 8, 8
L = 128
ITERS = 3
EPS = 1e-6
CHUNKS = 4
ROWS = 1024 // CHUNKS
PIECE = ROWS // 16


def coords():
    dp = lax.axis_index("dp")
    return lax.axis_index("proto"), (dp // 2) % Y, dp // (2 * Y), dp % 2


def device(x, y, z, c):
    return ((z * Y + y) * 2 + c, x)


def across(row):
    return jnp.transpose(jnp.broadcast_to(row, (L, L)))


def down(block):
    return jnp.sum(jnp.transpose(block), axis=0, keepdims=True)


def fold(block):
    return jnp.sum(block.reshape(-1, 8, block.shape[-1]), axis=0)


def unit(wide):
    return (wide * lax.rsqrt(jnp.sum(wide * wide, axis=-1, keepdims=True) + EPS)).astype(BF16)


def dot_t(a, b):
    return lax.dot_general(a, b, (((1,), (1,)), ((), ())), preferred_element_type=F32)


def copy_to(src, dst, send_sem, recv_sem, target):
    return pltpu.make_async_remote_copy(
        src, dst, send_sem, recv_sem, device_id=target, device_id_type=MESH
    )


def bytes_of(ref, sem):
    pltpu.make_async_copy(ref, ref, sem).wait()


def kernel(
    view_ref, slot_ref, proto_ref, loss_ref, grad_ref,
    view, slot, raw, unit_c, z_own, z_mine, z_other, expo, soft, weighted, z_scaled, grad_soft,
    col_wide, col_part, col_got, col_scale, row_part, row_got, row_scale, row_sum, more_part, more_got,
    half_send, half_got, half_own, half_out, piece_got, shard, whole, loss_rows, loss_send, loss_got,
    in_sem, z_send, z_recv, o_send, o_recv, col_ssem, col_rsem, row_ssem, row_rsem,
    more_ssem, more_rsem, half_ssem, half_rsem, piece_ssem, piece_rsem, all_ssem, all_rsem,
    near_ssem, near_rsem, pass_ssem, pass_rsem, loss_ssem, loss_rsem, out_sem,
):
    x, y, z, c = coords()
    yb, zb, yh, zh = y % 2, z % 2, y // 2, z // 2
    quad = zb * 2 + yb
    row_me = (x * 2 + yb) * 2 + zb
    col_me = zh * (Y // 2) + yh
    n_row, n_col = X * 4, (Y // 2) * (Z // 2)
    sibling = device(x, y, z, 1 - c)

    def row_peer(step):
        t = (row_me + step) % n_row
        return device(t // 4, yh * 2 + (t // 2) % 2, zh * 2 + t % 2, c)

    def col_peer(step):
        t = (col_me + step) % n_col
        return t, device(x, (t % (Y // 2)) * 2 + yb, (t // (Y // 2)) * 2 + zb, c)

    def block_chip(kind):
        return (yb + kind % 2) % 2, (zb + kind // 2) % 2

    def block_peer(kind, core):
        py, pz = block_chip(kind)
        return device(x, yh * 2 + py, zh * 2 + pz, core)

    def block_quad(kind):
        py, pz = block_chip(kind)
        return pz * 2 + py

    def near(dy, dz):
        return device(x, (y + dy) % Y, (z + dz) % Z, c)

    near_steps = [(1, 0), (-1, 0), (0, 1), (0, -1), (1, 1), (1, -1), (-1, 1), (-1, -1)]

    barrier = pltpu.get_barrier_semaphore()

    def hail(target):
        pl.semaphore_signal(barrier, inc=1, device_id=target, device_id_type=MESH)

    fetches = [
        pltpu.make_async_copy(slot_ref, slot, in_sem.at[0]),
        pltpu.make_async_copy(view_ref, view, in_sem.at[1]),
        pltpu.make_async_copy(proto_ref.at[pl.ds(quad * 2048, 2048)], raw, in_sem.at[2]),
    ]
    for fetch in fetches:
        fetch.start()

    def hail_groups(step, unused):
        hail(col_peer(step)[1])
        hail(row_peer(step))
        return unused

    lax.fori_loop(1, 16, hail_groups, 0)
    for dy, dz in near_steps:
        hail(near(dy, dz))
    for kind in range(1, 4):
        hail(block_peer(kind, 0))
        hail(block_peer(kind, 1))
    hail(sibling)

    fetches[0].wait()
    fetches[1].wait()
    lanes = lax.broadcasted_iota(jnp.int32, (L, 2 * L), 1).astype(F32)
    slots = slot[...].astype(F32)
    for v in range(2):
        chosen = across(slots[v : v + 1])
        pick = (jnp.concatenate([chosen, chosen], axis=1) == lanes).astype(F32).astype(BF16)
        z_own[v] = unit(jnp.dot(pick, view[...], preferred_element_type=F32))
    pl.semaphore_wait(barrier, 45)

    place = quad * 2 + c
    copy_to(z_own.at[1 - c], z_mine.at[place], z_send.at[0], z_recv.at[0], sibling).start()
    for kind in range(1, 4):
        for core in range(2):
            copy_to(
                z_own.at[core], z_mine.at[place], z_send.at[kind], z_recv.at[kind],
                block_peer(kind, core),
            ).start()
    z_mine[place] = z_own[c]
    fetches[2].wait()

    def normalise(b, unused):
        rows = pl.ds(b * 256, 256)
        unit_c[rows] = unit(raw[rows].astype(F32))
        return unused

    lax.fori_loop(0, 8, normalise, 0)

    def send_columns(it, h):
        def send(step, unused):
            copy_to(
                col_part.at[it, h], col_got.at[it, h, col_me], col_ssem.at[it, h],
                col_rsem.at[it, h], col_peer(step)[1],
            ).start()
            return unused

        lax.fori_loop(1, n_col, send, 0)
        col_got[it, h, col_me] = col_part[it, h]

    def wait_columns(it, h):
        bytes_of(col_got.at[it, h, pl.ds(0, n_col - 1)], col_rsem.at[it, h])
        total = col_got[it, h, 0]
        for m in range(1, n_col):
            total = total + col_got[it, h, m]
        col_scale[h] = 1.0 / total

    def first_block(q, rows_z, b):
        rows = pl.ds(b * 256, 256)
        scores = dot_t(unit_c[rows], rows_z)
        power = jnp.exp2(scores * (10.0 / math.log(2.0)))
        square = power * power
        soft[q, rows] = power.astype(BF16)
        expo[q, rows] = square
        return rows, square[:, :L] + square[:, L:], fold(power)

    for kind in range(4):
        q = block_quad(kind)
        got = z_mine.at[pl.ds(q * 2, 2)]
        bytes_of(z_mine.at[0] if kind == 0 else got, z_recv.at[kind])
        rows_z = z_mine[pl.ds(q * 2, 2)].reshape(256, L)

        def first(b, total, q=q, rows_z=rows_z, kind=kind):
            rows, wide, terms = first_block(q, rows_z, b)
            if kind == 0:
                col_wide[rows] = wide
            else:
                col_wide[rows] += wide
            return total + terms

        def first_last(b, total, q=q, rows_z=rows_z, h=0):
            rows, wide, terms = first_block(q, rows_z, h * 4 + b)
            wide = wide + col_wide[rows]
            col_part[0, h, pl.ds(b * 2, 1)] = down(wide[:L])
            col_part[0, h, pl.ds(b * 2 + 1, 1)] = down(wide[L:])
            return total + terms

        total = jnp.zeros((8, 256), F32)
        if kind < 3:
            total = lax.fori_loop(0, 8, first, total, unroll=2)
        else:
            for h in range(2):
                total = lax.fori_loop(
                    0, 4, lambda b, t, h=h: first_last(b, t, h=h), total, unroll=2
                )
                send_columns(0, h)
        terms = jnp.sum(total, axis=0, keepdims=True)
        more_part[0, pl.ds(q * 2, 1)] = terms[:, :L]
        more_part[0, pl.ds(q * 2 + 1, 1)] = terms[:, L:]

    for kind in range(4):
        bytes_of(z_mine.at[pl.ds(0, 1 if kind == 0 else 2)], z_send.at[kind])
    to_other = copy_to(z_mine, z_other, o_send, o_recv, sibling)
    to_other.start()

    def send_rows(part, got, ssem, rsem):
        def send(step, unused):
            copy_to(part, got.at[row_me], ssem, rsem, row_peer(step)).start()
            return unused

        lax.fori_loop(1, n_row, send, 0)
        got[row_me] = part[...]

    def wait_rows(got, rsem):
        bytes_of(got.at[pl.ds(0, n_row - 1)], rsem)
        total = got[0]
        for m in range(1, n_row):
            total = total + got[m]
        return total

    def row_pass(it, keep):
        acc = [jnp.zeros((8, 256), F32)] * 4
        for h in range(2):
            wait_columns(it, h)

            def step(b, acc, h=h):
                rows = pl.ds(h * 1024 + b * L, L)
                scale = across(col_scale[h, pl.ds(b, 1)])
                scale = jnp.concatenate([scale, scale], axis=1)
                new = []
                for q in range(4):
                    here = expo[q, rows] * scale
                    if keep:
                        weighted[q, rows] = here.astype(BF16)
                    new.append(acc[q] + fold(here))
                return new

            acc = lax.fori_loop(0, 8, step, acc, unroll=4)
        for q in range(4):
            sums = jnp.sum(acc[q], axis=0, keepdims=True)
            row_part[it, q * 2 : q * 2 + 1] = sums[:, :L]
            row_part[it, q * 2 + 1 : q * 2 + 2] = sums[:, L:]
        send_rows(row_part.at[it], row_got.at[it], row_ssem.at[it], row_rsem.at[it])

    def col_pass(it):
        for h in range(2):

            def step(b, unused, h=h):
                rows = pl.ds(h * 1024 + b * L, L)
                wide = None
                for q in range(4):
                    for s in range(2):
                        term = expo[q, rows, s * L : (s + 1) * L] * row_scale[2 * q + s : 2 * q + s + 1]
                        wide = term if wide is None else wide + term
                col_part[it, h, pl.ds(b, 1)] = down(wide)
                return unused

            lax.fori_loop(0, 8, step, 0, unroll=4)
            send_columns(it, h)

    row_pass(0, False)
    send_rows(more_part.at[0], more_got.at[0], more_ssem.at[0], more_rsem.at[0])
    row_scale[...] = 1.0 / wait_rows(row_got.at[0], row_rsem.at[0])
    col_pass(1)

    spread = wait_rows(more_got.at[0], more_rsem.at[0])
    loss_rows[0] = jnp.log(spread)
    gain = 10.0 / spread
    for t in range(8):
        z_scaled[t] = (z_mine[t].astype(F32) * across(gain[t : t + 1])).astype(BF16)

    def blocks_dot(left, rows):
        out = None
        for q in range(4):
            part = jnp.dot(
                left[q, rows], z_scaled[2 * q : 2 * q + 2].reshape(256, L), preferred_element_type=F32
            )
            out = part if out is None else out + part
        return out

    def soft_grad(b, unused):
        rows = pl.ds(b * 256, 256)
        grad_soft[rows] = blocks_dot(soft, rows)
        return unused

    lax.fori_loop(0, 8, soft_grad, 0)

    row_pass(1, False)
    row_scale[...] = 1.0 / wait_rows(row_got.at[1], row_rsem.at[1])
    col_pass(2)
    to_other.wait()
    row_pass(2, True)

    rows_o = [z_other[2 * q : 2 * q + 2].reshape(256, L) for q in range(4)]

    def cross_step(b, acc):
        rows = pl.ds(b * L, L)
        return [
            acc[q] + fold(weighted[q, rows].astype(F32) * dot_t(unit_c[rows], rows_o[q]))
            for q in range(4)
        ]

    acc = lax.fori_loop(0, 16, cross_step, [jnp.zeros((8, 256), F32)] * 4, unroll=2)
    for q in range(4):
        sums = jnp.sum(acc[q], axis=0, keepdims=True)
        more_part[1, q * 2 : q * 2 + 1] = sums[:, :L]
        more_part[1, q * 2 + 1 : q * 2 + 2] = sums[:, L:]
    row_total = wait_rows(row_got.at[2], row_rsem.at[2])
    scale = 1.0 / row_total
    row_scale[...] = scale
    row_sum[...] = row_total

    gain = scale * 10.0
    for t in range(8):
        z_scaled[t] = (z_other[t].astype(F32) * across(gain[t : t + 1])).astype(BF16)

    def grad_block(start):
        rows = pl.ds(start, ROWS)
        return grad_soft[rows] - blocks_dot(weighted, rows)

    def half_copy(m):
        return copy_to(half_send.at[m], half_got.at[m], half_ssem.at[m], half_rsem.at[m], sibling)

    def away(m):
        half_send[m] = grad_block((1 - c) * 1024 + m * ROWS).astype(BF16)
        half_copy(m).start()

    def stay(m):
        half_own[m] = grad_block(c * 1024 + m * ROWS)

    def scatter(m):
        half_copy(m).wait()
        both = half_own[m] + half_got[m].astype(F32)
        half_out[m] = both.astype(BF16).reshape(16, PIECE, L)

        def send(step, unused):
            t, target = col_peer(step)
            copy_to(
                half_out.at[m, t], piece_got.at[m, col_me], piece_ssem.at[m], piece_rsem.at[m], target
            ).start()
            return unused

        lax.fori_loop(1, n_col, send, 0)
        piece_got[m, col_me] = half_out[m, col_me]

    away(0)
    for m in range(CHUNKS):
        if m + 1 < CHUNKS:
            away(m + 1)
        stay(m)
        scatter(m)

    send_rows(more_part.at[1], more_got.at[1], more_ssem.at[1], more_rsem.at[1])
    cross = wait_rows(more_got.at[1], more_rsem.at[1])
    loss_rows[1] = row_scale[...] * cross
    loss_rows[2] = row_scale[...] * row_sum[...]
    theirs = pl.ds(quad * 2 + (1 - c), 1)
    loss_send[...] = jnp.zeros((8, L), F32)
    for n in range(3):
        loss_send[n : n + 1] = loss_rows[n, theirs]
    loss_copy = copy_to(loss_send, loss_got, loss_ssem, loss_rsem, sibling)
    loss_copy.start()

    def at_place(spot, m, start, count):
        return whole.at[spot, pl.ds(m * ROWS + start, count)]

    for m in range(CHUNKS):
        bytes_of(piece_got.at[m, pl.ds(0, n_col - 1)], piece_rsem.at[m])
        summed = piece_got[m, 0].astype(F32)
        for n in range(1, n_col):
            summed = summed + piece_got[m, n].astype(F32)
        shard[m] = summed.astype(BF16)

        def send_shard(step, unused, m=m):
            copy_to(
                shard.at[m], at_place(place, m, col_me * PIECE, PIECE), all_ssem.at[m],
                all_rsem.at[m], col_peer(step)[1],
            ).start()
            return unused

        lax.fori_loop(1, n_col, send_shard, 0)
        whole[place, pl.ds(m * ROWS + col_me * PIECE, PIECE)] = shard[m]

    loss_copy.wait()
    mine = pl.ds(place, 1)
    own_log, own_cross, own_mass = [loss_rows[n, mine] for n in range(3)]
    sib_log, sib_cross, sib_mass = [loss_got[n : n + 1] for n in range(3)]
    loss_ref[...] = -0.5 * (
        (own_cross + sib_cross) * 10.0 - own_log * sib_mass - sib_log * own_mass
    )

    kinds = [1, 1, 2, 2, 3, 3, 3, 3]
    half, fourth = ROWS // 2, ROWS // 4
    starts = [0, half, 0, half, 0, fourth, 2 * fourth, 3 * fourth]

    def hand_over(spot, m, kind):
        part = at_place(spot, m, 0, ROWS)
        copy_to(part, part, pass_ssem.at[kind, m], pass_rsem.at[kind, m], sibling).start()

    def write_out(spot, m):
        pltpu.make_async_copy(
            at_place(spot, m, 0, ROWS),
            grad_ref.at[pl.ds(spot * 1024 + m * ROWS, ROWS)],
            out_sem.at[spot, m],
        ).start()

    for m in range(CHUNKS):
        bytes_of(at_place(place, m, 0, ROWS - PIECE), all_rsem.at[m])
        for (dy, dz), kind, start in zip(near_steps, kinds, starts):
            part = at_place(place, m, start, fourth if kind == 3 else half)
            copy_to(
                part, part, near_ssem.at[kind - 1, m], near_rsem.at[kind - 1, m], near(dy, dz)
            ).start()
        hand_over(place, m, 0)
        write_out(place, m)
    for m in range(CHUNKS):
        for kind in range(1, 4):
            spot = block_quad(kind) * 2 + c
            bytes_of(at_place(spot, m, 0, ROWS), near_rsem.at[kind - 1, m])
            hand_over(spot, m, kind)
            write_out(spot, m)
    for m in range(CHUNKS):
        for kind in range(4):
            spot = block_quad(kind) * 2 + (1 - c)
            bytes_of(at_place(spot, m, 0, ROWS), pass_rsem.at[kind, m])
            write_out(spot, m)

    for m in range(CHUNKS):
        one = at_place(0, 0, 0, ROWS)
        for n in range(8):
            bytes_of(one, out_sem.at[n, m])
        for kind in range(4):
            bytes_of(one, pass_ssem.at[kind, m])
        for kind in range(3):
            bytes_of(one, near_ssem.at[kind, m])
        bytes_of(at_place(0, 0, 0, ROWS - PIECE), all_ssem.at[m])
        bytes_of(piece_got.at[m, pl.ds(0, n_col - 1)], piece_ssem.at[m])
    for it in range(ITERS):
        for h in range(2):
            bytes_of(col_got.at[it, h, pl.ds(0, n_col - 1)], col_ssem.at[it, h])
        bytes_of(row_got.at[it, pl.ds(0, n_row - 1)], row_ssem.at[it])
    for n in range(2):
        bytes_of(more_got.at[n, pl.ds(0, n_row - 1)], more_ssem.at[n])


def local(view_embed, pair_slot, prototypes):
    vmem, dma = pltpu.VMEM, pltpu.SemaphoreType.DMA
    scratch = [
        vmem((256, L), BF16),
        vmem((2, L), jnp.int32),
        vmem((2048, L), BF16),
        vmem((2048, L), BF16),
        vmem((2, L, L), BF16),
        vmem((8, L, L), BF16),
        vmem((8, L, L), BF16),
        vmem((4, 2048, 256), F32),
        vmem((4, 2048, 256), BF16),
        vmem((4, 2048, 256), BF16),
        vmem((8, L, L), BF16),
        vmem((2048, L), F32),
        vmem((2048, L), F32),
        vmem((ITERS, 2, 8, L), F32),
        vmem((ITERS, 2, 16, 8, L), F32),
        vmem((2, 8, L), F32),
        vmem((ITERS, 8, L), F32),
        vmem((ITERS, 16, 8, L), F32),
        vmem((8, L), F32),
        vmem((8, L), F32),
        vmem((2, 8, L), F32),
        vmem((2, 16, 8, L), F32),
        vmem((CHUNKS, ROWS, L), BF16),
        vmem((CHUNKS, ROWS, L), BF16),
        vmem((CHUNKS, ROWS, L), F32),
        vmem((CHUNKS, 16, PIECE, L), BF16),
        vmem((CHUNKS, 16, PIECE, L), BF16),
        vmem((CHUNKS, PIECE, L), BF16),
        vmem((8, 1024, L), BF16),
        vmem((3, 8, L), F32),
        vmem((8, L), F32),
        vmem((8, L), F32),
        dma((3,)), dma((4,)), dma((4,)), dma, dma,
        dma((ITERS, 2)), dma((ITERS, 2)), dma((ITERS,)), dma((ITERS,)),
        dma((2,)), dma((2,)),
        dma((CHUNKS,)), dma((CHUNKS,)), dma((CHUNKS,)), dma((CHUNKS,)),
        dma((CHUNKS,)), dma((CHUNKS,)),
        dma((3, CHUNKS)), dma((3, CHUNKS)), dma((4, CHUNKS)), dma((4, CHUNKS)),
        dma, dma, dma((8, CHUNKS)),
    ]
    loss, grad = pl.pallas_call(
        kernel,
        out_shape=[
            jax.ShapeDtypeStruct((1, L), F32),
            jax.ShapeDtypeStruct((8192, L), BF16),
        ],
        in_specs=[pl.BlockSpec(memory_space=pltpu.HBM)] * 3,
        out_specs=[
            pl.BlockSpec(memory_space=pltpu.VMEM),
            pl.BlockSpec(memory_space=pl.ANY),
        ],
        scratch_shapes=scratch,
        compiler_params=pltpu.CompilerParams(
            collective_id=0, has_side_effects=True, vmem_limit_bytes=50 << 20
        ),
        name="swav_step",
    )(view_embed, pair_slot.T, prototypes)
    return loss.reshape(L), grad


def solution(mesh):
    placed = (P("dp", None), P("dp", None), P("proto", None))
    return jax.shard_map(
        local, mesh=mesh, in_specs=placed, out_specs=(P("dp"), P("proto", None)), check_vma=False
    )
```

```python
import math

import jax
import jax.numpy as jnp
from jax import lax
from jax.experimental import pallas as pl
from jax.experimental.pallas import tpu as pltpu
from jax.sharding import PartitionSpec as P

MESH = pl.DeviceIdType.MESH
F32 = jnp.float32
BF16 = jnp.bfloat16
X, Y, Z = 4, 8, 8
L = 128
ITERS = 3
EPS = 1e-6
CHUNKS = 4
ROWS = 1024 // CHUNKS
PIECE = ROWS // 16


def coords():
    dp = lax.axis_index("dp")
    return lax.axis_index("proto"), (dp // 2) % Y, dp // (2 * Y), dp % 2


def device(x, y, z, c):
    return ((z * Y + y) * 2 + c, x)


def across(row):
    return jnp.transpose(jnp.broadcast_to(row, (L, L)))


def down(block):
    return jnp.sum(jnp.transpose(block), axis=0, keepdims=True)


def fold(block):
    return jnp.sum(block.reshape(-1, 8, block.shape[-1]), axis=0)


def unit(wide):
    return (wide * lax.rsqrt(jnp.sum(wide * wide, axis=-1, keepdims=True) + EPS)).astype(BF16)


def dot_t(a, b):
    return lax.dot_general(a, b, (((1,), (1,)), ((), ())), preferred_element_type=F32)


def copy_to(src, dst, send_sem, recv_sem, target):
    return pltpu.make_async_remote_copy(
        src, dst, send_sem, recv_sem, device_id=target, device_id_type=MESH
    )


def bytes_of(ref, sem):
    pltpu.make_async_copy(ref, ref, sem).wait()


def kernel(
    view_ref, slot_ref, proto_ref, loss_ref, grad_ref,
    view, slot, raw, unit_c, z_own, z_mine, z_other, expo, soft, weighted, z_scaled, grad_soft,
    col_wide, col_part, col_got, col_scale, row_part, row_got, row_scale, row_sum, more_part, more_got,
    half_send, half_got, half_own, half_out, piece_got, shard, loss_rows, loss_send, loss_got,
    here_sem, in_sem, z_send, z_recv, o_send, o_recv, col_ssem, col_rsem, row_ssem, row_rsem,
    more_ssem, more_rsem, half_ssem, half_rsem, piece_ssem, piece_rsem, all_ssem, all_rsem,
    near_ssem, near_rsem, pass_ssem, pass_rsem, loss_ssem, loss_rsem, out_sem,
):
    x, y, z, c = coords()
    yb, zb, yh, zh = y % 2, z % 2, y // 2, z // 2
    quad = zb * 2 + yb
    row_me = (x * 2 + yb) * 2 + zb
    col_me = zh * (Y // 2) + yh
    n_row, n_col = X * 4, (Y // 2) * (Z // 2)
    sibling = device(x, y, z, 1 - c)

    def wrap(value, size):
        return jnp.where(value >= size, value - size, value)

    z_far = [wrap(z + 2 * k, Z) * (2 * Y) for k in range(Z // 2)]
    y_far = [wrap(y + 2 * k, Y) * 2 + c for k in range(Y // 2)]
    z_place = [wrap(zh + k, Z // 2) * (Y // 2) for k in range(Z // 2)]
    y_place = [wrap(yh + k, Y // 2) for k in range(Y // 2)]
    x_all = [wrap(x + k, X) for k in range(X)]
    z_near = [z * (2 * Y), (z + 1 - 2 * zb) * (2 * Y)]
    y_near = [y * 2 + c, (y + 1 - 2 * yb) * 2 + c]

    col_peers = [
        (z_place[i] + y_place[j], (z_far[i] + y_far[j], x))
        for i, j in sorted(
            ((i, j) for i in range(4) for j in range(4) if i or j),
            key=lambda p: -min(p[0], 4 - p[0]) - min(p[1], 4 - p[1]),
        )
    ]
    row_peers = [
        (z_near[i] + y_near[j], x_all[k])
        for k in (2, 1, 3, 0)
        for i in range(2)
        for j in range(2)
        if i or j or k
    ]

    def block_chip(kind):
        return (yb + kind % 2) % 2, (zb + kind // 2) % 2

    def block_peer(kind, core):
        py, pz = block_chip(kind)
        return device(x, yh * 2 + py, zh * 2 + pz, core)

    def block_quad(kind):
        py, pz = block_chip(kind)
        return pz * 2 + py

    def near(dy, dz):
        return device(x, (y + dy) % Y, (z + dz) % Z, c)

    near_steps = [(1, 0), (-1, 0), (0, 1), (0, -1), (1, 1), (1, -1), (-1, 1), (-1, -1)]

    barrier = pltpu.get_barrier_semaphore()

    def hail(target):
        pl.semaphore_signal(barrier, inc=1, device_id=target, device_id_type=MESH)

    fetches = [
        pltpu.make_async_copy(slot_ref, slot, in_sem.at[0]),
        pltpu.make_async_copy(view_ref, view, in_sem.at[1]),
        pltpu.make_async_copy(proto_ref.at[pl.ds(quad * 2048, 2048)], raw, in_sem.at[2]),
    ]
    for fetch in fetches:
        fetch.start()

    along_y = [(z_far[0] + y_far[k], x) for k in (2, 1, 3)]
    along_z = [(z_far[k] + y_far[0], x) for k in (2, 1, 3)]
    along_x = [(z_near[0] + y_near[0], x_all[k]) for k in (2, 1, 3)]
    for target in along_y + along_z + along_x:
        hail(target)
    out_y, out_z = 2 * yb - 1, 2 * zb - 1
    for dy, dz in ((out_y, 0), (0, out_z), (out_y, out_z), (out_y, -out_z), (-out_y, out_z)):
        hail(near(dy, dz))
    for kind in range(1, 4):
        hail(block_peer(kind, 0))
        hail(block_peer(kind, 1))
    hail(sibling)

    fetches[0].wait()
    fetches[1].wait()
    lanes = lax.broadcasted_iota(jnp.int32, (L, 2 * L), 1).astype(F32)
    slots = slot[...].astype(F32)
    for v in range(2):
        chosen = across(slots[v : v + 1])
        pick = (jnp.concatenate([chosen, chosen], axis=1) == lanes).astype(F32).astype(BF16)
        z_own[v] = unit(jnp.dot(pick, view[...], preferred_element_type=F32))
    pl.semaphore_wait(barrier, 21)

    place = quad * 2 + c
    copy_to(z_own.at[1 - c], z_mine.at[place], z_send.at[0], z_recv.at[0], sibling).start()
    for kind in range(1, 4):
        for core in range(2):
            copy_to(
                z_own.at[core], z_mine.at[place], z_send.at[kind], z_recv.at[kind],
                block_peer(kind, core),
            ).start()
    for n, peers in enumerate((along_y, along_x)):
        for target in peers:
            pl.semaphore_signal(
                here_sem.at[n], inc=1, device_id=target, device_id_type=MESH
            )
    z_mine[place] = z_own[c]
    fetches[2].wait()

    def normalise(b, unused):
        rows = pl.ds(b * 256, 256)
        unit_c[rows] = unit(raw[rows].astype(F32))
        return unused

    lax.fori_loop(0, 8, normalise, 0)

    def send_columns(it, h):
        for _, target in col_peers:
            copy_to(
                col_part.at[it, h], col_got.at[it, h, col_me], col_ssem.at[it, h],
                col_rsem.at[it, h], target,
            ).start()
        col_got[it, h, col_me] = col_part[it, h]

    def wait_columns(it, h):
        bytes_of(col_got.at[it, h, pl.ds(0, n_col - 1)], col_rsem.at[it, h])
        total = col_got[it, h, 0]
        for m in range(1, n_col):
            total = total + col_got[it, h, m]
        col_scale[h] = 1.0 / total

    def first_block(q, rows_z, b):
        rows = pl.ds(b * 256, 256)
        scores = dot_t(unit_c[rows], rows_z)
        power = jnp.exp2(scores * (10.0 / math.log(2.0)))
        square = power * power
        soft[q, rows] = power.astype(BF16)
        expo[q, rows] = square
        return rows, square[:, :L] + square[:, L:], fold(power)

    for kind in range(4):
        q = block_quad(kind)
        got = z_mine.at[pl.ds(q * 2, 2)]
        bytes_of(z_mine.at[0] if kind == 0 else got, z_recv.at[kind])
        rows_z = z_mine[pl.ds(q * 2, 2)].reshape(256, L)

        def first(b, total, q=q, rows_z=rows_z, kind=kind):
            rows, wide, terms = first_block(q, rows_z, b)
            if kind == 0:
                col_wide[rows] = wide
            else:
                col_wide[rows] += wide
            return total + terms

        def first_last(b, total, q=q, rows_z=rows_z, h=0):
            rows, wide, terms = first_block(q, rows_z, h * 4 + b)
            wide = wide + col_wide[rows]
            col_part[0, h, pl.ds(b * 2, 1)] = down(wide[:L])
            col_part[0, h, pl.ds(b * 2 + 1, 1)] = down(wide[L:])
            return total + terms

        total = jnp.zeros((8, 256), F32)
        if kind == 3:
            pl.semaphore_wait(here_sem.at[0], 3)
            pl.semaphore_wait(here_sem.at[1], 3)
        if kind < 3:
            total = lax.fori_loop(0, 8, first, total, unroll=2)
        else:
            for h in range(2):
                total = lax.fori_loop(
                    0, 4, lambda b, t, h=h: first_last(b, t, h=h), total, unroll=2
                )
                send_columns(0, h)
        terms = jnp.sum(total, axis=0, keepdims=True)
        more_part[0, pl.ds(q * 2, 1)] = terms[:, :L]
        more_part[0, pl.ds(q * 2 + 1, 1)] = terms[:, L:]

    for kind in range(4):
        bytes_of(z_mine.at[pl.ds(0, 1 if kind == 0 else 2)], z_send.at[kind])
    to_other = copy_to(z_mine, z_other, o_send, o_recv, sibling)
    to_other.start()

    def send_rows(part, got, ssem, rsem):
        for target in row_peers:
            copy_to(part, got.at[row_me], ssem, rsem, target).start()
        got[row_me] = part[...]

    def wait_rows(got, rsem):
        bytes_of(got.at[pl.ds(0, n_row - 1)], rsem)
        total = got[0]
        for m in range(1, n_row):
            total = total + got[m]
        return total

    def row_pass(it, keep):
        acc = [jnp.zeros((8, 256), F32)] * 4
        for h in range(2):
            wait_columns(it, h)

            def step(b, acc, h=h):
                rows = pl.ds(h * 1024 + b * L, L)
                scale = across(col_scale[h, pl.ds(b, 1)])
                scale = jnp.concatenate([scale, scale], axis=1)
                new = []
                for q in range(4):
                    here = expo[q, rows] * scale
                    if keep:
                        weighted[q, rows] = here.astype(BF16)
                    new.append(acc[q] + fold(here))
                return new

            acc = lax.fori_loop(0, 8, step, acc, unroll=4)
        for q in range(4):
            sums = jnp.sum(acc[q], axis=0, keepdims=True)
            row_part[it, q * 2 : q * 2 + 1] = sums[:, :L]
            row_part[it, q * 2 + 1 : q * 2 + 2] = sums[:, L:]
        send_rows(row_part.at[it], row_got.at[it], row_ssem.at[it], row_rsem.at[it])

    def col_pass(it):
        for h in range(2):

            def step(b, unused, h=h):
                rows = pl.ds(h * 1024 + b * L, L)
                wide = None
                for q in range(4):
                    for s in range(2):
                        term = expo[q, rows, s * L : (s + 1) * L] * row_scale[2 * q + s : 2 * q + s + 1]
                        wide = term if wide is None else wide + term
                col_part[it, h, pl.ds(b, 1)] = down(wide)
                return unused

            lax.fori_loop(0, 8, step, 0, unroll=4)
            send_columns(it, h)

    row_pass(0, False)
    send_rows(more_part.at[0], more_got.at[0], more_ssem.at[0], more_rsem.at[0])
    row_scale[...] = 1.0 / wait_rows(row_got.at[0], row_rsem.at[0])
    col_pass(1)

    spread = wait_rows(more_got.at[0], more_rsem.at[0])
    loss_rows[0] = jnp.log(spread)
    gain = 10.0 / spread
    for t in range(8):
        z_scaled[t] = (z_mine[t].astype(F32) * across(gain[t : t + 1])).astype(BF16)

    def blocks_dot(left, rows):
        out = None
        for q in range(4):
            part = jnp.dot(
                left[q, rows], z_scaled[2 * q : 2 * q + 2].reshape(256, L), preferred_element_type=F32
            )
            out = part if out is None else out + part
        return out

    def soft_grad(b, unused):
        rows = pl.ds(b * 256, 256)
        grad_soft[rows] = blocks_dot(soft, rows)
        return unused

    lax.fori_loop(0, 8, soft_grad, 0)

    row_pass(1, False)
    row_scale[...] = 1.0 / wait_rows(row_got.at[1], row_rsem.at[1])
    col_pass(2)
    to_other.wait()
    row_pass(2, True)

    rows_o = [z_other[2 * q : 2 * q + 2].reshape(256, L) for q in range(4)]

    def cross_step(b, acc):
        rows = pl.ds(b * L, L)
        return [
            acc[q] + fold(weighted[q, rows].astype(F32) * dot_t(unit_c[rows], rows_o[q]))
            for q in range(4)
        ]

    acc = lax.fori_loop(0, 16, cross_step, [jnp.zeros((8, 256), F32)] * 4, unroll=2)
    for q in range(4):
        sums = jnp.sum(acc[q], axis=0, keepdims=True)
        more_part[1, q * 2 : q * 2 + 1] = sums[:, :L]
        more_part[1, q * 2 + 1 : q * 2 + 2] = sums[:, L:]
    row_total = wait_rows(row_got.at[2], row_rsem.at[2])
    scale = 1.0 / row_total
    row_scale[...] = scale
    row_sum[...] = row_total

    gain = scale * 10.0
    for t in range(8):
        z_scaled[t] = (z_other[t].astype(F32) * across(gain[t : t + 1])).astype(BF16)

    def grad_block(start):
        rows = pl.ds(start, ROWS)
        return grad_soft[rows] - blocks_dot(weighted, rows)

    def half_copy(m):
        return copy_to(half_send.at[m], half_got.at[m], half_ssem.at[m], half_rsem.at[m], sibling)

    def away(m):
        half_send[m] = grad_block((1 - c) * 1024 + m * ROWS).astype(BF16)
        half_copy(m).start()

    def stay(m):
        half_own[m] = grad_block(c * 1024 + m * ROWS)

    def scatter(m):
        half_copy(m).wait()
        both = half_own[m] + half_got[m].astype(F32)
        half_out[m] = both.astype(BF16).reshape(16, PIECE, L)

        for t, target in col_peers:
            copy_to(
                half_out.at[m, t], piece_got.at[m, col_me], piece_ssem.at[m], piece_rsem.at[m], target
            ).start()
        piece_got[m, col_me] = half_out[m, col_me]

    away(0)
    for m in range(CHUNKS):
        if m + 1 < CHUNKS:
            away(m + 1)
        stay(m)
        scatter(m)

    send_rows(more_part.at[1], more_got.at[1], more_ssem.at[1], more_rsem.at[1])
    cross = wait_rows(more_got.at[1], more_rsem.at[1])
    loss_rows[1] = row_scale[...] * cross
    loss_rows[2] = row_scale[...] * row_sum[...]
    theirs = pl.ds(quad * 2 + (1 - c), 1)
    loss_send[...] = jnp.zeros((8, L), F32)
    for n in range(3):
        loss_send[n : n + 1] = loss_rows[n, theirs]
    loss_copy = copy_to(loss_send, loss_got, loss_ssem, loss_rsem, sibling)
    loss_copy.start()

    def at_place(spot, m, start, count):
        return grad_ref.at[pl.ds(spot * 1024 + m * ROWS + start, count)]

    def own_copy(m):
        return pltpu.make_async_copy(
            shard.at[m], at_place(place, m, col_me * PIECE, PIECE), out_sem.at[m]
        )

    for m in range(CHUNKS):
        bytes_of(piece_got.at[m, pl.ds(0, n_col - 1)], piece_rsem.at[m])
        summed = piece_got[m, 0].astype(F32)
        for n in range(1, n_col):
            summed = summed + piece_got[m, n].astype(F32)
        shard[m] = summed.astype(BF16)

        for _, target in col_peers:
            copy_to(
                shard.at[m], at_place(place, m, col_me * PIECE, PIECE), all_ssem.at[m],
                all_rsem.at[m], target,
            ).start()
        own_copy(m).start()

    loss_copy.wait()
    mine = pl.ds(place, 1)
    own_log, own_cross, own_mass = [loss_rows[n, mine] for n in range(3)]
    sib_log, sib_cross, sib_mass = [loss_got[n : n + 1] for n in range(3)]
    loss_ref[...] = -0.5 * (
        (own_cross + sib_cross) * 10.0 - own_log * sib_mass - sib_log * own_mass
    )

    kinds = [1, 1, 2, 2, 3, 3, 3, 3]
    half, fourth = ROWS // 2, ROWS // 4
    starts = [0, half, 0, half, 0, fourth, 2 * fourth, 3 * fourth]

    def hand_over(spot, m, kind):
        part = at_place(spot, m, 0, ROWS)
        copy_to(part, part, pass_ssem.at[kind, m], pass_rsem.at[kind, m], sibling).start()

    for m in range(CHUNKS):
        own_copy(m).wait()
        bytes_of(at_place(place, m, 0, ROWS - PIECE), all_rsem.at[m])
        for (dy, dz), kind, start in zip(near_steps, kinds, starts):
            part = at_place(place, m, start, fourth if kind == 3 else half)
            copy_to(
                part, part, near_ssem.at[kind - 1, m], near_rsem.at[kind - 1, m], near(dy, dz)
            ).start()
        hand_over(place, m, 0)
    for m in range(CHUNKS):
        for kind in range(1, 4):
            spot = block_quad(kind) * 2 + c
            bytes_of(at_place(spot, m, 0, ROWS), near_rsem.at[kind - 1, m])
            hand_over(spot, m, kind)
    for m in range(CHUNKS):
        for kind in range(4):
            spot = block_quad(kind) * 2 + (1 - c)
            bytes_of(at_place(spot, m, 0, ROWS), pass_rsem.at[kind, m])

    for m in range(CHUNKS):
        one = at_place(0, 0, 0, ROWS)
        for kind in range(4):
            bytes_of(one, pass_ssem.at[kind, m])
        for kind in range(3):
            bytes_of(one, near_ssem.at[kind, m])
        bytes_of(at_place(0, 0, 0, ROWS - PIECE), all_ssem.at[m])
        bytes_of(piece_got.at[m, pl.ds(0, n_col - 1)], piece_ssem.at[m])
    for it in range(ITERS):
        for h in range(2):
            bytes_of(col_got.at[it, h, pl.ds(0, n_col - 1)], col_ssem.at[it, h])
        bytes_of(row_got.at[it, pl.ds(0, n_row - 1)], row_ssem.at[it])
    for n in range(2):
        bytes_of(more_got.at[n, pl.ds(0, n_row - 1)], more_ssem.at[n])


def local(view_embed, pair_slot, prototypes):
    vmem, dma = pltpu.VMEM, pltpu.SemaphoreType.DMA
    scratch = [
        vmem((256, L), BF16),
        vmem((2, L), jnp.int32),
        vmem((2048, L), BF16),
        vmem((2048, L), BF16),
        vmem((2, L, L), BF16),
        vmem((8, L, L), BF16),
        vmem((8, L, L), BF16),
        vmem((4, 2048, 256), F32),
        vmem((4, 2048, 256), BF16),
        vmem((4, 2048, 256), BF16),
        vmem((8, L, L), BF16),
        vmem((2048, L), F32),
        vmem((2048, L), F32),
        vmem((ITERS, 2, 8, L), F32),
        vmem((ITERS, 2, 16, 8, L), F32),
        vmem((2, 8, L), F32),
        vmem((ITERS, 8, L), F32),
        vmem((ITERS, 16, 8, L), F32),
        vmem((8, L), F32),
        vmem((8, L), F32),
        vmem((2, 8, L), F32),
        vmem((2, 16, 8, L), F32),
        vmem((CHUNKS, ROWS, L), BF16),
        vmem((CHUNKS, ROWS, L), BF16),
        vmem((CHUNKS, ROWS, L), F32),
        vmem((CHUNKS, 16, PIECE, L), BF16),
        vmem((CHUNKS, 16, PIECE, L), BF16),
        vmem((CHUNKS, PIECE, L), BF16),
        vmem((3, 8, L), F32),
        vmem((8, L), F32),
        vmem((8, L), F32),
        pltpu.SemaphoreType.REGULAR((2,)),
        dma((3,)), dma((4,)), dma((4,)), dma, dma,
        dma((ITERS, 2)), dma((ITERS, 2)), dma((ITERS,)), dma((ITERS,)),
        dma((2,)), dma((2,)),
        dma((CHUNKS,)), dma((CHUNKS,)), dma((CHUNKS,)), dma((CHUNKS,)),
        dma((CHUNKS,)), dma((CHUNKS,)),
        dma((3, CHUNKS)), dma((3, CHUNKS)), dma((4, CHUNKS)), dma((4, CHUNKS)),
        dma, dma, dma((CHUNKS,)),
    ]
    loss, grad = pl.pallas_call(
        kernel,
        out_shape=[
            jax.ShapeDtypeStruct((1, L), F32),
            jax.ShapeDtypeStruct((8192, L), BF16),
        ],
        in_specs=[pl.BlockSpec(memory_space=pltpu.HBM)] * 3,
        out_specs=[
            pl.BlockSpec(memory_space=pltpu.VMEM),
            pl.BlockSpec(memory_space=pl.ANY),
        ],
        scratch_shapes=scratch,
        compiler_params=pltpu.CompilerParams(
            collective_id=0, has_side_effects=True, vmem_limit_bytes=50 << 20
        ),
        name="swav_step",
    )(view_embed, pair_slot.T, prototypes)
    return loss.reshape(L), grad


def solution(mesh):
    placed = (P("dp", None), P("dp", None), P("proto", None))
    return jax.shard_map(
        local, mesh=mesh, in_specs=placed, out_specs=(P("dp"), P("proto", None)), check_vma=False
    )
```

```python
import math

import jax
import jax.numpy as jnp
from jax import lax
from jax.experimental import pallas as pl
from jax.experimental.pallas import tpu as pltpu
from jax.sharding import PartitionSpec as P

MESH = pl.DeviceIdType.MESH
F32 = jnp.float32
BF16 = jnp.bfloat16
X, Y, Z = 4, 8, 8
L = 128
ITERS = 3
EPS = 1e-6
CHUNKS = 4
ROWS = 1024 // CHUNKS
PIECE = ROWS // 16


def coords():
    dp = lax.axis_index("dp")
    return lax.axis_index("proto"), (dp // 2) % Y, dp // (2 * Y), dp % 2


def device(x, y, z, c):
    return ((z * Y + y) * 2 + c, x)


def across(row):
    return jnp.transpose(jnp.broadcast_to(row, (L, L)))


def down(block):
    return jnp.sum(jnp.transpose(block), axis=0, keepdims=True)


def fold(block):
    return jnp.sum(block.reshape(-1, 8, block.shape[-1]), axis=0)


def unit(wide):
    return (wide * lax.rsqrt(jnp.sum(wide * wide, axis=-1, keepdims=True) + EPS)).astype(BF16)


def dot_t(a, b):
    return lax.dot_general(a, b, (((1,), (1,)), ((), ())), preferred_element_type=F32)


def copy_to(src, dst, send_sem, recv_sem, target):
    return pltpu.make_async_remote_copy(
        src, dst, send_sem, recv_sem, device_id=target, device_id_type=MESH
    )


def bytes_of(ref, sem):
    pltpu.make_async_copy(ref, ref, sem).wait()


def kernel(
    view_ref, slot_ref, proto_ref, loss_ref, grad_ref,
    view, slot, raw, unit_c, z_own, z_mine, z_other, expo, soft, weighted, z_scaled, grad_soft,
    col_wide, col_part, col_got, col_scale, row_part, row_got, row_scale, row_sum, more_part, more_got,
    half_send, half_got, half_own, half_out, piece_got, shard, loss_rows, loss_send, loss_got,
    here_sem, in_sem, z_send, z_recv, o_send, o_recv, col_ssem, col_rsem, row_ssem, row_rsem,
    more_ssem, more_rsem, half_ssem, half_rsem, piece_ssem, piece_rsem, all_ssem, all_rsem,
    near_ssem, near_rsem, pass_ssem, pass_rsem, loss_ssem, loss_rsem, out_sem,
):
    x, y, z, c = coords()
    yb, zb, yh, zh = y % 2, z % 2, y // 2, z // 2
    quad = zb * 2 + yb
    row_me = (x * 2 + yb) * 2 + zb
    col_me = zh * (Y // 2) + yh
    n_row, n_col = X * 4, (Y // 2) * (Z // 2)
    sibling = device(x, y, z, 1 - c)

    def wrap(value, size):
        return jnp.where(value >= size, value - size, value)

    z_far = [wrap(z + 2 * k, Z) * (2 * Y) for k in range(Z // 2)]
    y_far = [wrap(y + 2 * k, Y) * 2 + c for k in range(Y // 2)]
    z_place = [wrap(zh + k, Z // 2) * (Y // 2) for k in range(Z // 2)]
    y_place = [wrap(yh + k, Y // 2) for k in range(Y // 2)]
    x_all = [wrap(x + k, X) for k in range(X)]
    z_near = [z * (2 * Y), (z + 1 - 2 * zb) * (2 * Y)]
    y_near = [y * 2 + c, (y + 1 - 2 * yb) * 2 + c]

    col_peers = [
        (z_place[i] + y_place[j], (z_far[i] + y_far[j], x))
        for i, j in sorted(
            ((i, j) for i in range(4) for j in range(4) if i or j),
            key=lambda p: -min(p[0], 4 - p[0]) - min(p[1], 4 - p[1]),
        )
    ]
    row_peers = [
        (z_near[i] + y_near[j], x_all[k])
        for k in (2, 1, 3, 0)
        for i in range(2)
        for j in range(2)
        if i or j or k
    ]

    def block_chip(kind):
        return (yb + kind % 2) % 2, (zb + kind // 2) % 2

    def block_peer(kind, core):
        py, pz = block_chip(kind)
        return device(x, yh * 2 + py, zh * 2 + pz, core)

    def block_quad(kind):
        py, pz = block_chip(kind)
        return pz * 2 + py

    def near(dy, dz):
        return device(x, (y + dy) % Y, (z + dz) % Z, c)

    near_steps = [(1, 0), (-1, 0), (0, 1), (0, -1), (1, 1), (1, -1), (-1, 1), (-1, -1)]

    barrier = pltpu.get_barrier_semaphore()

    def hail(target):
        pl.semaphore_signal(barrier, inc=1, device_id=target, device_id_type=MESH)

    fetches = [
        pltpu.make_async_copy(slot_ref, slot, in_sem.at[0]),
        pltpu.make_async_copy(view_ref, view, in_sem.at[1]),
        pltpu.make_async_copy(proto_ref.at[pl.ds(quad * 2048, 2048)], raw, in_sem.at[2]),
    ]
    for fetch in fetches:
        fetch.start()

    along_y = [(z_far[0] + y_far[k], x) for k in (2, 1, 3)]
    along_z = [(z_far[k] + y_far[0], x) for k in (2, 1, 3)]
    along_x = [(z_near[0] + y_near[0], x_all[k]) for k in (2, 1, 3)]
    for target in along_y + along_z + along_x:
        hail(target)
    out_y, out_z = 2 * yb - 1, 2 * zb - 1
    for dy, dz in ((out_y, 0), (0, out_z), (out_y, out_z), (out_y, -out_z), (-out_y, out_z)):
        hail(near(dy, dz))
    for kind in range(1, 4):
        hail(block_peer(kind, 0))
        hail(block_peer(kind, 1))
    hail(sibling)

    fetches[0].wait()
    fetches[1].wait()
    lanes = lax.broadcasted_iota(jnp.int32, (L, 2 * L), 1).astype(F32)
    slots = slot[...].astype(F32)
    for v in range(2):
        chosen = across(slots[v : v + 1])
        pick = (jnp.concatenate([chosen, chosen], axis=1) == lanes).astype(F32).astype(BF16)
        z_own[v] = unit(jnp.dot(pick, view[...], preferred_element_type=F32))
    pl.semaphore_wait(barrier, 21)

    place = quad * 2 + c
    copy_to(z_own.at[1 - c], z_mine.at[place], z_send.at[0], z_recv.at[0], sibling).start()
    for kind in range(1, 4):
        for core in range(2):
            copy_to(
                z_own.at[core], z_mine.at[place], z_send.at[kind], z_recv.at[kind],
                block_peer(kind, core),
            ).start()
    for n, peers in enumerate((along_y, along_x)):
        for target in peers:
            pl.semaphore_signal(
                here_sem.at[n], inc=1, device_id=target, device_id_type=MESH
            )
    z_mine[place] = z_own[c]
    fetches[2].wait()

    def normalise(b, unused):
        rows = pl.ds(b * 256, 256)
        unit_c[rows] = unit(raw[rows].astype(F32))
        return unused

    lax.fori_loop(0, 8, normalise, 0, unroll=2)

    def send_columns(it, h):
        for _, target in col_peers:
            copy_to(
                col_part.at[it, h], col_got.at[it, h, col_me], col_ssem.at[it, h],
                col_rsem.at[it, h], target,
            ).start()
        col_got[it, h, col_me] = col_part[it, h]

    def wait_columns(it, h):
        bytes_of(col_got.at[it, h, pl.ds(0, n_col - 1)], col_rsem.at[it, h])
        total = col_got[it, h, 0]
        for m in range(1, n_col):
            total = total + col_got[it, h, m]
        col_scale[h] = 1.0 / total

    def first_block(q, rows_z, b):
        rows = pl.ds(b * 256, 256)
        scores = dot_t(unit_c[rows], rows_z)
        power = jnp.exp2(scores * (10.0 / math.log(2.0)))
        square = power * power
        soft[q, rows] = power.astype(BF16)
        expo[q, rows] = square
        return rows, square[:, :L] + square[:, L:], fold(power)

    for kind in range(4):
        q = block_quad(kind)
        got = z_mine.at[pl.ds(q * 2, 2)]
        bytes_of(z_mine.at[0] if kind == 0 else got, z_recv.at[kind])
        rows_z = z_mine[pl.ds(q * 2, 2)].reshape(256, L)

        def first(b, total, q=q, rows_z=rows_z, kind=kind):
            rows, wide, terms = first_block(q, rows_z, b)
            if kind == 0:
                col_wide[rows] = wide
            else:
                col_wide[rows] += wide
            return total + terms

        def first_last(b, total, q=q, rows_z=rows_z, h=0):
            rows, wide, terms = first_block(q, rows_z, h * 4 + b)
            wide = wide + col_wide[rows]
            col_part[0, h, pl.ds(b * 2, 1)] = down(wide[:L])
            col_part[0, h, pl.ds(b * 2 + 1, 1)] = down(wide[L:])
            return total + terms

        total = jnp.zeros((8, 256), F32)
        if kind == 3:
            pl.semaphore_wait(here_sem.at[0], 3)
            pl.semaphore_wait(here_sem.at[1], 3)
        if kind < 3:
            total = lax.fori_loop(0, 8, first, total, unroll=4)
        else:
            for h in range(2):
                total = lax.fori_loop(
                    0, 4, lambda b, t, h=h: first_last(b, t, h=h), total, unroll=4
                )
                send_columns(0, h)
        terms = jnp.sum(total, axis=0, keepdims=True)
        more_part[0, pl.ds(q * 2, 1)] = terms[:, :L]
        more_part[0, pl.ds(q * 2 + 1, 1)] = terms[:, L:]

    for kind in range(4):
        bytes_of(z_mine.at[pl.ds(0, 1 if kind == 0 else 2)], z_send.at[kind])
    to_other = copy_to(z_mine, z_other, o_send, o_recv, sibling)
    to_other.start()

    def send_rows(part, got, ssem, rsem):
        for target in row_peers:
            copy_to(part, got.at[row_me], ssem, rsem, target).start()
        got[row_me] = part[...]

    def wait_rows(got, rsem):
        bytes_of(got.at[pl.ds(0, n_row - 1)], rsem)
        total = got[0]
        for m in range(1, n_row):
            total = total + got[m]
        return total

    def row_pass(it, keep):
        acc = [jnp.zeros((8, 256), F32)] * 4
        for h in range(2):
            wait_columns(it, h)

            def step(b, acc, h=h):
                rows = pl.ds(h * 1024 + b * L, L)
                scale = across(col_scale[h, pl.ds(b, 1)])
                scale = jnp.concatenate([scale, scale], axis=1)
                new = []
                for q in range(4):
                    here = expo[q, rows] * scale
                    if keep:
                        weighted[q, rows] = here.astype(BF16)
                    new.append(acc[q] + fold(here))
                return new

            acc = lax.fori_loop(0, 8, step, acc, unroll=8)
        for q in range(4):
            sums = jnp.sum(acc[q], axis=0, keepdims=True)
            row_part[it, q * 2 : q * 2 + 1] = sums[:, :L]
            row_part[it, q * 2 + 1 : q * 2 + 2] = sums[:, L:]
        send_rows(row_part.at[it], row_got.at[it], row_ssem.at[it], row_rsem.at[it])

    def col_pass(it):
        for h in range(2):

            def step(b, unused, h=h):
                rows = pl.ds(h * 1024 + b * L, L)
                wide = None
                for q in range(4):
                    for s in range(2):
                        term = expo[q, rows, s * L : (s + 1) * L] * row_scale[2 * q + s : 2 * q + s + 1]
                        wide = term if wide is None else wide + term
                col_part[it, h, pl.ds(b, 1)] = down(wide)
                return unused

            lax.fori_loop(0, 8, step, 0, unroll=8)
            send_columns(it, h)

    row_pass(0, False)
    send_rows(more_part.at[0], more_got.at[0], more_ssem.at[0], more_rsem.at[0])
    row_scale[...] = 1.0 / wait_rows(row_got.at[0], row_rsem.at[0])
    col_pass(1)

    spread = wait_rows(more_got.at[0], more_rsem.at[0])
    loss_rows[0] = jnp.log(spread)
    gain = 10.0 / spread
    for t in range(8):
        z_scaled[t] = (z_mine[t].astype(F32) * across(gain[t : t + 1])).astype(BF16)

    def blocks_dot(left, rows):
        out = None
        for q in range(4):
            part = jnp.dot(
                left[q, rows], z_scaled[2 * q : 2 * q + 2].reshape(256, L), preferred_element_type=F32
            )
            out = part if out is None else out + part
        return out

    def soft_grad(b, unused):
        rows = pl.ds(b * 256, 256)
        grad_soft[rows] = blocks_dot(soft, rows)
        return unused

    lax.fori_loop(0, 8, soft_grad, 0)

    row_pass(1, False)
    row_scale[...] = 1.0 / wait_rows(row_got.at[1], row_rsem.at[1])
    col_pass(2)
    to_other.wait()
    row_pass(2, True)

    rows_o = [z_other[2 * q : 2 * q + 2].reshape(256, L) for q in range(4)]

    def cross_step(b, acc):
        rows = pl.ds(b * L, L)
        return [
            acc[q] + fold(weighted[q, rows].astype(F32) * dot_t(unit_c[rows], rows_o[q]))
            for q in range(4)
        ]

    acc = lax.fori_loop(0, 16, cross_step, [jnp.zeros((8, 256), F32)] * 4, unroll=2)
    for q in range(4):
        sums = jnp.sum(acc[q], axis=0, keepdims=True)
        more_part[1, q * 2 : q * 2 + 1] = sums[:, :L]
        more_part[1, q * 2 + 1 : q * 2 + 2] = sums[:, L:]
    row_total = wait_rows(row_got.at[2], row_rsem.at[2])
    scale = 1.0 / row_total
    row_scale[...] = scale
    row_sum[...] = row_total

    gain = scale * 10.0
    for t in range(8):
        z_scaled[t] = (z_other[t].astype(F32) * across(gain[t : t + 1])).astype(BF16)

    def grad_block(start):
        rows = pl.ds(start, ROWS)
        return grad_soft[rows] - blocks_dot(weighted, rows)

    def half_copy(m):
        return copy_to(half_send.at[m], half_got.at[m], half_ssem.at[m], half_rsem.at[m], sibling)

    def away(m):
        half_send[m] = grad_block((1 - c) * 1024 + m * ROWS).astype(BF16)
        half_copy(m).start()

    def stay(m):
        half_own[m] = grad_block(c * 1024 + m * ROWS)

    def scatter(m):
        half_copy(m).wait()
        both = half_own[m] + half_got[m].astype(F32)
        half_out[m] = both.astype(BF16).reshape(16, PIECE, L)

        for t, target in col_peers:
            copy_to(
                half_out.at[m, t], piece_got.at[m, col_me], piece_ssem.at[m], piece_rsem.at[m], target
            ).start()
        piece_got[m, col_me] = half_out[m, col_me]

    for m in range(CHUNKS):
        away(m)
    for m in range(CHUNKS):
        stay(m)
        scatter(m)

    send_rows(more_part.at[1], more_got.at[1], more_ssem.at[1], more_rsem.at[1])
    cross = wait_rows(more_got.at[1], more_rsem.at[1])
    loss_rows[1] = row_scale[...] * cross
    loss_rows[2] = row_scale[...] * row_sum[...]
    theirs = pl.ds(quad * 2 + (1 - c), 1)
    loss_send[...] = jnp.zeros((8, L), F32)
    for n in range(3):
        loss_send[n : n + 1] = loss_rows[n, theirs]
    loss_copy = copy_to(loss_send, loss_got, loss_ssem, loss_rsem, sibling)
    loss_copy.start()

    def at_place(spot, m, start, count):
        return grad_ref.at[pl.ds(spot * 1024 + m * ROWS + start, count)]

    def own_copy(m):
        return pltpu.make_async_copy(
            shard.at[m], at_place(place, m, col_me * PIECE, PIECE), out_sem.at[m]
        )

    for m in range(CHUNKS):
        bytes_of(piece_got.at[m, pl.ds(0, n_col - 1)], piece_rsem.at[m])
        summed = piece_got[m, 0].astype(F32)
        for n in range(1, n_col):
            summed = summed + piece_got[m, n].astype(F32)
        shard[m] = summed.astype(BF16)

        for _, target in col_peers:
            copy_to(
                shard.at[m], at_place(place, m, col_me * PIECE, PIECE), all_ssem.at[m],
                all_rsem.at[m], target,
            ).start()
        own_copy(m).start()

    loss_copy.wait()
    mine = pl.ds(place, 1)
    own_log, own_cross, own_mass = [loss_rows[n, mine] for n in range(3)]
    sib_log, sib_cross, sib_mass = [loss_got[n : n + 1] for n in range(3)]
    loss_ref[...] = -0.5 * (
        (own_cross + sib_cross) * 10.0 - own_log * sib_mass - sib_log * own_mass
    )

    kinds = [1, 1, 2, 2, 3, 3, 3, 3]
    half, fourth = ROWS // 2, ROWS // 4
    starts = [0, half, 0, half, 0, fourth, 2 * fourth, 3 * fourth]

    def hand_over(spot, m, kind):
        part = at_place(spot, m, 0, ROWS)
        copy_to(part, part, pass_ssem.at[kind, m], pass_rsem.at[kind, m], sibling).start()

    for m in range(CHUNKS):
        own_copy(m).wait()
        bytes_of(at_place(place, m, 0, ROWS - PIECE), all_rsem.at[m])
        for (dy, dz), kind, start in zip(near_steps, kinds, starts):
            part = at_place(place, m, start, fourth if kind == 3 else half)
            copy_to(
                part, part, near_ssem.at[kind - 1, m], near_rsem.at[kind - 1, m], near(dy, dz)
            ).start()
        hand_over(place, m, 0)
    for m in range(CHUNKS):
        for kind in range(1, 4):
            spot = block_quad(kind) * 2 + c
            bytes_of(at_place(spot, m, 0, ROWS), near_rsem.at[kind - 1, m])
            hand_over(spot, m, kind)
    for m in range(CHUNKS):
        for kind in range(4):
            spot = block_quad(kind) * 2 + (1 - c)
            bytes_of(at_place(spot, m, 0, ROWS), pass_rsem.at[kind, m])

    for m in range(CHUNKS):
        one = at_place(0, 0, 0, ROWS)
        for kind in range(4):
            bytes_of(one, pass_ssem.at[kind, m])
        for kind in range(3):
            bytes_of(one, near_ssem.at[kind, m])
        bytes_of(at_place(0, 0, 0, ROWS - PIECE), all_ssem.at[m])
        bytes_of(piece_got.at[m, pl.ds(0, n_col - 1)], piece_ssem.at[m])
    for it in range(ITERS):
        for h in range(2):
            bytes_of(col_got.at[it, h, pl.ds(0, n_col - 1)], col_ssem.at[it, h])
        bytes_of(row_got.at[it, pl.ds(0, n_row - 1)], row_ssem.at[it])
    for n in range(2):
        bytes_of(more_got.at[n, pl.ds(0, n_row - 1)], more_ssem.at[n])


def local(view_embed, pair_slot, prototypes):
    vmem, dma = pltpu.VMEM, pltpu.SemaphoreType.DMA
    scratch = [
        vmem((256, L), BF16),
        vmem((2, L), jnp.int32),
        vmem((2048, L), BF16),
        vmem((2048, L), BF16),
        vmem((2, L, L), BF16),
        vmem((8, L, L), BF16),
        vmem((8, L, L), BF16),
        vmem((4, 2048, 256), F32),
        vmem((4, 2048, 256), BF16),
        vmem((4, 2048, 256), BF16),
        vmem((8, L, L), BF16),
        vmem((2048, L), F32),
        vmem((2048, L), F32),
        vmem((ITERS, 2, 8, L), F32),
        vmem((ITERS, 2, 16, 8, L), F32),
        vmem((2, 8, L), F32),
        vmem((ITERS, 8, L), F32),
        vmem((ITERS, 16, 8, L), F32),
        vmem((8, L), F32),
        vmem((8, L), F32),
        vmem((2, 8, L), F32),
        vmem((2, 16, 8, L), F32),
        vmem((CHUNKS, ROWS, L), BF16),
        vmem((CHUNKS, ROWS, L), BF16),
        vmem((CHUNKS, ROWS, L), F32),
        vmem((CHUNKS, 16, PIECE, L), BF16),
        vmem((CHUNKS, 16, PIECE, L), BF16),
        vmem((CHUNKS, PIECE, L), BF16),
        vmem((3, 8, L), F32),
        vmem((8, L), F32),
        vmem((8, L), F32),
        pltpu.SemaphoreType.REGULAR((2,)),
        dma((3,)), dma((4,)), dma((4,)), dma, dma,
        dma((ITERS, 2)), dma((ITERS, 2)), dma((ITERS,)), dma((ITERS,)),
        dma((2,)), dma((2,)),
        dma((CHUNKS,)), dma((CHUNKS,)), dma((CHUNKS,)), dma((CHUNKS,)),
        dma((CHUNKS,)), dma((CHUNKS,)),
        dma((3, CHUNKS)), dma((3, CHUNKS)), dma((4, CHUNKS)), dma((4, CHUNKS)),
        dma, dma, dma((CHUNKS,)),
    ]
    loss, grad = pl.pallas_call(
        kernel,
        out_shape=[
            jax.ShapeDtypeStruct((1, L), F32),
            jax.ShapeDtypeStruct((8192, L), BF16),
        ],
        in_specs=[pl.BlockSpec(memory_space=pltpu.HBM)] * 3,
        out_specs=[
            pl.BlockSpec(memory_space=pltpu.VMEM),
            pl.BlockSpec(memory_space=pl.ANY),
        ],
        scratch_shapes=scratch,
        compiler_params=pltpu.CompilerParams(
            collective_id=0, has_side_effects=True, vmem_limit_bytes=50 << 20
        ),
        name="swav_step",
    )(view_embed, pair_slot.T, prototypes)
    return loss.reshape(L), grad


def solution(mesh):
    placed = (P("dp", None), P("dp", None), P("proto", None))
    return jax.shard_map(
        local, mesh=mesh, in_specs=placed, out_specs=(P("dp"), P("proto", None)), check_vma=False
    )
```

```python
import math

import jax
import jax.numpy as jnp
from jax import lax
from jax.experimental import pallas as pl
from jax.experimental.pallas import tpu as pltpu
from jax.sharding import PartitionSpec as P

MESH = pl.DeviceIdType.MESH
F32 = jnp.float32
BF16 = jnp.bfloat16
X, Y, Z = 4, 8, 8
L = 128
ITERS = 3
EPS = 1e-6
CHUNKS = 4
ROWS = 1024 // CHUNKS
PIECE = ROWS // 16


def coords():
    dp = lax.axis_index("dp")
    return lax.axis_index("proto"), (dp // 2) % Y, dp // (2 * Y), dp % 2


def device(x, y, z, c):
    return ((z * Y + y) * 2 + c, x)


def across(row):
    return jnp.transpose(jnp.broadcast_to(row, (L, L)))


def down(block):
    return jnp.sum(jnp.transpose(block), axis=0, keepdims=True)


def fold(block):
    return jnp.sum(block.reshape(-1, 8, block.shape[-1]), axis=0)


def unit(wide):
    return (wide * lax.rsqrt(jnp.sum(wide * wide, axis=-1, keepdims=True) + EPS)).astype(BF16)


def dot_t(a, b):
    return lax.dot_general(a, b, (((1,), (1,)), ((), ())), preferred_element_type=F32)


def copy_to(src, dst, send_sem, recv_sem, target):
    return pltpu.make_async_remote_copy(
        src, dst, send_sem, recv_sem, device_id=target, device_id_type=MESH
    )


def bytes_of(ref, sem):
    pltpu.make_async_copy(ref, ref, sem).wait()


def kernel(
    view_ref, slot_ref, proto_ref, loss_ref, grad_ref,
    view, slot, raw, unit_c, z_own, z_mine, z_other, expo, soft, weighted, z_scaled, grad_soft,
    col_wide, col_part, col_got, col_scale, row_part, row_got, row_scale, row_sum, more_part, more_got,
    half_send, half_got, half_own, half_out, piece_got, shard, loss_rows, loss_send, loss_got,
    here_sem, in_sem, z_send, z_recv, o_send, o_recv, col_ssem, col_rsem, row_ssem, row_rsem,
    more_ssem, more_rsem, half_ssem, half_rsem, piece_ssem, piece_rsem, all_ssem, all_rsem,
    near_ssem, near_rsem, pass_ssem, pass_rsem, loss_ssem, loss_rsem, out_sem,
):
    x, y, z, c = coords()
    yb, zb, yh, zh = y % 2, z % 2, y // 2, z // 2
    quad = zb * 2 + yb
    row_me = (x * 2 + yb) * 2 + zb
    col_me = zh * (Y // 2) + yh
    n_row, n_col = X * 4, (Y // 2) * (Z // 2)
    sibling = device(x, y, z, 1 - c)

    def wrap(value, size):
        return jnp.where(value >= size, value - size, value)

    z_far = [wrap(z + 2 * k, Z) * (2 * Y) for k in range(Z // 2)]
    y_far = [wrap(y + 2 * k, Y) * 2 + c for k in range(Y // 2)]
    z_place = [wrap(zh + k, Z // 2) * (Y // 2) for k in range(Z // 2)]
    y_place = [wrap(yh + k, Y // 2) for k in range(Y // 2)]
    x_all = [wrap(x + k, X) for k in range(X)]
    z_near = [z * (2 * Y), (z + 1 - 2 * zb) * (2 * Y)]
    y_near = [y * 2 + c, (y + 1 - 2 * yb) * 2 + c]

    col_peers = [
        (z_place[i] + y_place[j], (z_far[i] + y_far[j], x))
        for i, j in sorted(
            ((i, j) for i in range(4) for j in range(4) if i or j),
            key=lambda p: -min(p[0], 4 - p[0]) - min(p[1], 4 - p[1]),
        )
    ]
    row_peers = [
        (z_near[i] + y_near[j], x_all[k])
        for k in (2, 1, 3, 0)
        for i in range(2)
        for j in range(2)
        if i or j or k
    ]

    def block_chip(kind):
        return (yb + kind % 2) % 2, (zb + kind // 2) % 2

    def block_peer(kind, core):
        py, pz = block_chip(kind)
        return device(x, yh * 2 + py, zh * 2 + pz, core)

    def block_quad(kind):
        py, pz = block_chip(kind)
        return pz * 2 + py

    def near(dy, dz):
        return device(x, (y + dy) % Y, (z + dz) % Z, c)

    near_steps = [(1, 0), (-1, 0), (0, 1), (0, -1), (1, 1), (1, -1), (-1, 1), (-1, -1)]

    barrier = pltpu.get_barrier_semaphore()

    def hail(target):
        pl.semaphore_signal(barrier, inc=1, device_id=target, device_id_type=MESH)

    fetches = [
        pltpu.make_async_copy(slot_ref, slot, in_sem.at[0]),
        pltpu.make_async_copy(view_ref, view, in_sem.at[1]),
        pltpu.make_async_copy(proto_ref.at[pl.ds(quad * 2048, 2048)], raw, in_sem.at[2]),
    ]
    for fetch in fetches:
        fetch.start()

    along_y = [(z_far[0] + y_far[k], x) for k in (2, 1, 3)]
    along_z = [(z_far[k] + y_far[0], x) for k in (2, 1, 3)]
    along_x = [(z_near[0] + y_near[0], x_all[k]) for k in (2, 1, 3)]
    for target in along_y + along_z + along_x:
        hail(target)
    out_y, out_z = 2 * yb - 1, 2 * zb - 1
    for dy, dz in ((out_y, 0), (0, out_z), (out_y, out_z), (out_y, -out_z), (-out_y, out_z)):
        hail(near(dy, dz))
    for kind in range(1, 4):
        hail(block_peer(kind, 0))
        hail(block_peer(kind, 1))
    hail(sibling)

    fetches[0].wait()
    fetches[1].wait()
    lanes = lax.broadcasted_iota(jnp.int32, (L, 2 * L), 1).astype(F32)
    slots = slot[...].astype(F32)
    for v in range(2):
        chosen = across(slots[v : v + 1])
        pick = (jnp.concatenate([chosen, chosen], axis=1) == lanes).astype(F32).astype(BF16)
        z_own[v] = unit(jnp.dot(pick, view[...], preferred_element_type=F32))
    pl.semaphore_wait(barrier, 21)

    place = quad * 2 + c
    copy_to(z_own.at[1 - c], z_mine.at[place], z_send.at[0], z_recv.at[0], sibling).start()
    for kind in range(1, 4):
        for core in range(2):
            copy_to(
                z_own.at[core], z_mine.at[place], z_send.at[kind], z_recv.at[kind],
                block_peer(kind, core),
            ).start()
    for n, peers in enumerate((along_y, along_x)):
        for target in peers:
            pl.semaphore_signal(
                here_sem.at[n], inc=1, device_id=target, device_id_type=MESH
            )
    z_mine[place] = z_own[c]
    fetches[2].wait()

    def normalise(b, unused):
        rows = pl.ds(b * 256, 256)
        unit_c[rows] = unit(raw[rows].astype(F32))
        return unused

    lax.fori_loop(0, 8, normalise, 0, unroll=4)

    def send_columns(it, h):
        for _, target in col_peers:
            copy_to(
                col_part.at[it, h], col_got.at[it, h, col_me], col_ssem.at[it, h],
                col_rsem.at[it, h], target,
            ).start()
        col_got[it, h, col_me] = col_part[it, h]

    def wait_columns(it, h):
        bytes_of(col_got.at[it, h, pl.ds(0, n_col - 1)], col_rsem.at[it, h])
        total = col_got[it, h, 0]
        for m in range(1, n_col):
            total = total + col_got[it, h, m]
        col_scale[h] = 1.0 / total

    def first_block(q, rows_z, b):
        rows = pl.ds(b * 256, 256)
        scores = dot_t(unit_c[rows], rows_z)
        power = jnp.exp2(scores * (10.0 / math.log(2.0)))
        square = power * power
        soft[q, rows] = power.astype(BF16)
        expo[q, rows] = square
        return rows, square[:, :L] + square[:, L:], fold(power)

    for kind in range(4):
        q = block_quad(kind)
        got = z_mine.at[pl.ds(q * 2, 2)]
        bytes_of(z_mine.at[0] if kind == 0 else got, z_recv.at[kind])
        rows_z = z_mine[pl.ds(q * 2, 2)].reshape(256, L)

        def first(b, total, q=q, rows_z=rows_z, kind=kind):
            rows, wide, terms = first_block(q, rows_z, b)
            if kind == 0:
                col_wide[rows] = wide
            else:
                col_wide[rows] += wide
            return total + terms

        def first_last(b, total, q=q, rows_z=rows_z, h=0):
            rows, wide, terms = first_block(q, rows_z, h * 4 + b)
            wide = wide + col_wide[rows]
            col_part[0, h, pl.ds(b * 2, 1)] = down(wide[:L])
            col_part[0, h, pl.ds(b * 2 + 1, 1)] = down(wide[L:])
            return total + terms

        total = jnp.zeros((8, 256), F32)
        if kind == 3:
            pl.semaphore_wait(here_sem.at[0], 3)
            pl.semaphore_wait(here_sem.at[1], 3)
        if kind < 3:
            total = lax.fori_loop(0, 8, first, total, unroll=8)
        else:
            for h in range(2):
                total = lax.fori_loop(
                    0, 4, lambda b, t, h=h: first_last(b, t, h=h), total, unroll=4
                )
                send_columns(0, h)
        terms = jnp.sum(total, axis=0, keepdims=True)
        more_part[0, pl.ds(q * 2, 1)] = terms[:, :L]
        more_part[0, pl.ds(q * 2 + 1, 1)] = terms[:, L:]

    for kind in range(4):
        bytes_of(z_mine.at[pl.ds(0, 1 if kind == 0 else 2)], z_send.at[kind])
    to_other = copy_to(z_mine, z_other, o_send, o_recv, sibling)
    to_other.start()

    def send_rows(part, got, ssem, rsem):
        for target in row_peers:
            copy_to(part, got.at[row_me], ssem, rsem, target).start()
        got[row_me] = part[...]

    def wait_rows(got, rsem):
        bytes_of(got.at[pl.ds(0, n_row - 1)], rsem)
        total = got[0]
        for m in range(1, n_row):
            total = total + got[m]
        return total

    def row_pass(it, keep):
        acc = [jnp.zeros((8, 256), F32)] * 4
        for h in range(2):
            wait_columns(it, h)

            def step(b, acc, h=h):
                rows = pl.ds(h * 1024 + b * L, L)
                scale = across(col_scale[h, pl.ds(b, 1)])
                scale = jnp.concatenate([scale, scale], axis=1)
                new = []
                for q in range(4):
                    here = expo[q, rows] * scale
                    if keep:
                        weighted[q, rows] = here.astype(BF16)
                    new.append(acc[q] + fold(here))
                return new

            acc = lax.fori_loop(0, 8, step, acc, unroll=8)
        for q in range(4):
            sums = jnp.sum(acc[q], axis=0, keepdims=True)
            row_part[it, q * 2 : q * 2 + 1] = sums[:, :L]
            row_part[it, q * 2 + 1 : q * 2 + 2] = sums[:, L:]
        send_rows(row_part.at[it], row_got.at[it], row_ssem.at[it], row_rsem.at[it])

    def col_pass(it):
        for h in range(2):

            def step(b, unused, h=h):
                rows = pl.ds(h * 1024 + b * L, L)
                wide = None
                for q in range(4):
                    for s in range(2):
                        term = expo[q, rows, s * L : (s + 1) * L] * row_scale[2 * q + s : 2 * q + s + 1]
                        wide = term if wide is None else wide + term
                col_part[it, h, pl.ds(b, 1)] = down(wide)
                return unused

            lax.fori_loop(0, 8, step, 0, unroll=8)
            send_columns(it, h)

    row_pass(0, False)
    send_rows(more_part.at[0], more_got.at[0], more_ssem.at[0], more_rsem.at[0])
    row_scale[...] = 1.0 / wait_rows(row_got.at[0], row_rsem.at[0])
    col_pass(1)

    spread = wait_rows(more_got.at[0], more_rsem.at[0])
    loss_rows[0] = jnp.log(spread)
    gain = 10.0 / spread
    for t in range(8):
        z_scaled[t] = (z_mine[t].astype(F32) * across(gain[t : t + 1])).astype(BF16)

    def blocks_dot(left, rows):
        out = None
        for q in range(4):
            part = jnp.dot(
                left[q, rows], z_scaled[2 * q : 2 * q + 2].reshape(256, L), preferred_element_type=F32
            )
            out = part if out is None else out + part
        return out

    def soft_grad(b, unused):
        rows = pl.ds(b * 256, 256)
        grad_soft[rows] = blocks_dot(soft, rows)
        return unused

    lax.fori_loop(0, 8, soft_grad, 0)

    row_pass(1, False)
    row_scale[...] = 1.0 / wait_rows(row_got.at[1], row_rsem.at[1])
    col_pass(2)
    to_other.wait()
    row_pass(2, True)

    rows_o = [z_other[2 * q : 2 * q + 2].reshape(256, L) for q in range(4)]

    def cross_step(b, acc):
        rows = pl.ds(b * L, L)
        return [
            acc[q] + fold(weighted[q, rows].astype(F32) * dot_t(unit_c[rows], rows_o[q]))
            for q in range(4)
        ]

    acc = lax.fori_loop(0, 16, cross_step, [jnp.zeros((8, 256), F32)] * 4, unroll=2)
    for q in range(4):
        sums = jnp.sum(acc[q], axis=0, keepdims=True)
        more_part[1, q * 2 : q * 2 + 1] = sums[:, :L]
        more_part[1, q * 2 + 1 : q * 2 + 2] = sums[:, L:]
    row_total = wait_rows(row_got.at[2], row_rsem.at[2])
    scale = 1.0 / row_total
    row_scale[...] = scale
    row_sum[...] = row_total

    gain = scale * 10.0
    for t in range(8):
        z_scaled[t] = (z_other[t].astype(F32) * across(gain[t : t + 1])).astype(BF16)

    def grad_block(start):
        rows = pl.ds(start, ROWS)
        return grad_soft[rows] - blocks_dot(weighted, rows)

    def half_copy(m):
        return copy_to(half_send.at[m], half_got.at[m], half_ssem.at[m], half_rsem.at[m], sibling)

    def away(m):
        half_send[m] = grad_block((1 - c) * 1024 + m * ROWS).astype(BF16)
        half_copy(m).start()

    def stay(m):
        half_own[m] = grad_block(c * 1024 + m * ROWS)

    def scatter(m):
        half_copy(m).wait()
        both = half_own[m] + half_got[m].astype(F32)
        half_out[m] = both.astype(BF16).reshape(16, PIECE, L)

        for t, target in col_peers:
            copy_to(
                half_out.at[m, t], piece_got.at[m, col_me], piece_ssem.at[m], piece_rsem.at[m], target
            ).start()
        piece_got[m, col_me] = half_out[m, col_me]

    for m in range(CHUNKS):
        away(m)
    for m in range(CHUNKS):
        stay(m)
        scatter(m)

    send_rows(more_part.at[1], more_got.at[1], more_ssem.at[1], more_rsem.at[1])
    cross = wait_rows(more_got.at[1], more_rsem.at[1])
    loss_rows[1] = row_scale[...] * cross
    loss_rows[2] = row_scale[...] * row_sum[...]
    theirs = pl.ds(quad * 2 + (1 - c), 1)
    loss_send[...] = jnp.zeros((8, L), F32)
    for n in range(3):
        loss_send[n : n + 1] = loss_rows[n, theirs]
    loss_copy = copy_to(loss_send, loss_got, loss_ssem, loss_rsem, sibling)
    loss_copy.start()

    def at_place(spot, m, start, count):
        return grad_ref.at[pl.ds(spot * 1024 + m * ROWS + start, count)]

    def own_copy(m):
        return pltpu.make_async_copy(
            shard.at[m], at_place(place, m, col_me * PIECE, PIECE), out_sem.at[m]
        )

    for m in range(CHUNKS):
        bytes_of(piece_got.at[m, pl.ds(0, n_col - 1)], piece_rsem.at[m])
        summed = piece_got[m, 0].astype(F32)
        for n in range(1, n_col):
            summed = summed + piece_got[m, n].astype(F32)
        shard[m] = summed.astype(BF16)

        for _, target in col_peers:
            copy_to(
                shard.at[m], at_place(place, m, col_me * PIECE, PIECE), all_ssem.at[m],
                all_rsem.at[m], target,
            ).start()
        own_copy(m).start()

    loss_copy.wait()
    mine = pl.ds(place, 1)
    own_log, own_cross, own_mass = [loss_rows[n, mine] for n in range(3)]
    sib_log, sib_cross, sib_mass = [loss_got[n : n + 1] for n in range(3)]
    loss_ref[...] = -0.5 * (
        (own_cross + sib_cross) * 10.0 - own_log * sib_mass - sib_log * own_mass
    )

    kinds = [1, 1, 2, 2, 3, 3, 3, 3]
    half, fourth = ROWS // 2, ROWS // 4
    starts = [0, half, 0, half, 0, fourth, 2 * fourth, 3 * fourth]

    def hand_over(spot, m, kind):
        part = at_place(spot, m, 0, ROWS)
        copy_to(part, part, pass_ssem.at[kind, m], pass_rsem.at[kind, m], sibling).start()

    for m in range(CHUNKS):
        own_copy(m).wait()
        bytes_of(at_place(place, m, 0, ROWS - PIECE), all_rsem.at[m])
        for (dy, dz), kind, start in zip(near_steps, kinds, starts):
            part = at_place(place, m, start, fourth if kind == 3 else half)
            copy_to(
                part, part, near_ssem.at[kind - 1, m], near_rsem.at[kind - 1, m], near(dy, dz)
            ).start()
        hand_over(place, m, 0)
    for m in range(CHUNKS):
        for kind in range(1, 4):
            spot = block_quad(kind) * 2 + c
            bytes_of(at_place(spot, m, 0, ROWS), near_rsem.at[kind - 1, m])
            hand_over(spot, m, kind)
    for m in range(CHUNKS):
        for kind in range(4):
            spot = block_quad(kind) * 2 + (1 - c)
            bytes_of(at_place(spot, m, 0, ROWS), pass_rsem.at[kind, m])

    for m in range(CHUNKS):
        one = at_place(0, 0, 0, ROWS)
        for kind in range(4):
            bytes_of(one, pass_ssem.at[kind, m])
        for kind in range(3):
            bytes_of(one, near_ssem.at[kind, m])
        bytes_of(at_place(0, 0, 0, ROWS - PIECE), all_ssem.at[m])
        bytes_of(piece_got.at[m, pl.ds(0, n_col - 1)], piece_ssem.at[m])
    for it in range(ITERS):
        for h in range(2):
            bytes_of(col_got.at[it, h, pl.ds(0, n_col - 1)], col_ssem.at[it, h])
        bytes_of(row_got.at[it, pl.ds(0, n_row - 1)], row_ssem.at[it])
    for n in range(2):
        bytes_of(more_got.at[n, pl.ds(0, n_row - 1)], more_ssem.at[n])


def local(view_embed, pair_slot, prototypes):
    vmem, dma = pltpu.VMEM, pltpu.SemaphoreType.DMA
    scratch = [
        vmem((256, L), BF16),
        vmem((2, L), jnp.int32),
        vmem((2048, L), BF16),
        vmem((2048, L), BF16),
        vmem((2, L, L), BF16),
        vmem((8, L, L), BF16),
        vmem((8, L, L), BF16),
        vmem((4, 2048, 256), F32),
        vmem((4, 2048, 256), BF16),
        vmem((4, 2048, 256), BF16),
        vmem((8, L, L), BF16),
        vmem((2048, L), F32),
        vmem((2048, L), F32),
        vmem((ITERS, 2, 8, L), F32),
        vmem((ITERS, 2, 16, 8, L), F32),
        vmem((2, 8, L), F32),
        vmem((ITERS, 8, L), F32),
        vmem((ITERS, 16, 8, L), F32),
        vmem((8, L), F32),
        vmem((8, L), F32),
        vmem((2, 8, L), F32),
        vmem((2, 16, 8, L), F32),
        vmem((CHUNKS, ROWS, L), BF16),
        vmem((CHUNKS, ROWS, L), BF16),
        vmem((CHUNKS, ROWS, L), F32),
        vmem((CHUNKS, 16, PIECE, L), BF16),
        vmem((CHUNKS, 16, PIECE, L), BF16),
        vmem((CHUNKS, PIECE, L), BF16),
        vmem((3, 8, L), F32),
        vmem((8, L), F32),
        vmem((8, L), F32),
        pltpu.SemaphoreType.REGULAR((2,)),
        dma((3,)), dma((4,)), dma((4,)), dma, dma,
        dma((ITERS, 2)), dma((ITERS, 2)), dma((ITERS,)), dma((ITERS,)),
        dma((2,)), dma((2,)),
        dma((CHUNKS,)), dma((CHUNKS,)), dma((CHUNKS,)), dma((CHUNKS,)),
        dma((CHUNKS,)), dma((CHUNKS,)),
        dma((3, CHUNKS)), dma((3, CHUNKS)), dma((4, CHUNKS)), dma((4, CHUNKS)),
        dma, dma, dma((CHUNKS,)),
    ]
    loss, grad = pl.pallas_call(
        kernel,
        out_shape=[
            jax.ShapeDtypeStruct((1, L), F32),
            jax.ShapeDtypeStruct((8192, L), BF16),
        ],
        in_specs=[pl.BlockSpec(memory_space=pltpu.HBM)] * 3,
        out_specs=[
            pl.BlockSpec(memory_space=pltpu.VMEM),
            pl.BlockSpec(memory_space=pl.ANY),
        ],
        scratch_shapes=scratch,
        compiler_params=pltpu.CompilerParams(
            collective_id=0, has_side_effects=True, vmem_limit_bytes=50 << 20
        ),
        name="swav_step",
    )(view_embed, pair_slot.T, prototypes)
    return loss.reshape(L), grad


def solution(mesh):
    placed = (P("dp", None), P("dp", None), P("proto", None))
    return jax.shard_map(
        local, mesh=mesh, in_specs=placed, out_specs=(P("dp"), P("proto", None)), check_vma=False
    )
```
